512 devices in a mesh: ctx: 128 (over z, y, core), head: 4 (over x).
Axes of the slice: x: 4, y: 8, z: 8, core: 2. Of those that a mesh axis runs over, the one named last changes fastest.
Arguments:
- queries: bfloat16 [16384, 4096], P('ctx', 'head'), may hold values from -6 to 6
- keys: bfloat16 [16384, 4096], P('ctx', 'head'), may hold values from -6 to 6
- values: bfloat16 [16384, 4096], P('ctx', 'head'), may hold values from -6 to 6
- head_gain: float32 [4096], P('head'), may hold values from 0.5 to 1.5
- w_out: bfloat16 [4096, 4096], P('head', 'ctx'), may hold values from -0.09375 to 0.09375
Outputs:
- projected: bfloat16 [16384, 4096], P('ctx', 'head')
The draws below stay inside these ranges and needn't reach their ends.
All inputs are finite; a program needn't handle non-finite values.
Results may differ from the reference program's by a relative error of at most 0.013.
Values may be sent and summed in bfloat16 or wider, within the bound.
A program may use at most 192 MiB of HBM per device.

```python
import jax
import jax.numpy as jnp
from jax import lax

D = 4096
HEADS = 32
HD = 128
TOK_DEV = 128
TOKENS = 16384
N_CTX = 128
N_HEAD = 4


def shard_levels(stream_key, dims, shards, least, high):
    def one(position, blocks):
        steps = jax.random.uniform(jax.random.fold_in(jax.random.fold_in(stream_key, 6), position), (blocks,), jnp.float32, least / len(shards), high / len(shards))
        return jnp.repeat(jnp.exp(steps), dims[position] // blocks).reshape((-1,) + (1,) * (len(dims) - position - 1))

    loudness = one(*shards[0])
    for cut in shards[1:]:
        loudness = loudness * one(*cut)
    return loudness


def bell_draw(own_key, extent, spread, limit, split=(), kind=jnp.bfloat16):
    entries = spread * jax.random.normal(own_key, extent, jnp.float32)
    if split:
        entries = entries * shard_levels(own_key, extent, split, -0.22, 0.18)
    return jnp.clip(entries, -limit, limit).astype(kind)


def setup_inputs(seed: int = 0) -> dict:
    key_list = jax.random.split(jax.random.key(seed), 6)
    queries = bell_draw(key_list[0], (TOKENS, HEADS * HD), 1.0, 6.0, ((0, 128), (1, 4)))
    keys = bell_draw(key_list[1], (TOKENS, HEADS * HD), 1.0, 6.0, ((0, 128), (1, 4)))
    values = bell_draw(key_list[2], (TOKENS, HEADS * HD), 1.0, 6.0, ((0, 128), (1, 4)))
    head_gain = jnp.clip(0.5 + 1.0 * jax.random.uniform(key_list[3], (HEADS * HD,), jnp.float32) ** shard_levels(key_list[3], (HEADS * HD,), ((0, 4),), -0.2, 0.2), 0.5, 1.5)
    w_out = bell_draw(key_list[4], (HEADS * HD, D), (HEADS * HD) ** -0.5, 0.09375, ((0, 4), (1, 128)))
    return {"queries": queries, "keys": keys, "values": values, "head_gain": head_gain, "w_out": w_out}


def feature(x):
    return (jax.nn.elu(x.astype(jnp.float32)) + 1.0).astype(jnp.bfloat16)

def reference(queries, keys, values, head_gain, w_out):
    fq = feature(queries).reshape(N_CTX, TOK_DEV, HEADS, HD)
    fk = feature(keys).reshape(N_CTX, TOK_DEV, HEADS, HD)
    vals = values.reshape(N_CTX, TOK_DEV, HEADS, HD)
    gain = head_gain.reshape(HEADS, HD)
    rows = jnp.arange(TOK_DEV, dtype=jnp.int32)
    causal = rows[None, :, None] >= rows[None, None, :]
    group = HEADS * HD // N_HEAD

    def step(prefix, block):
        bq, bk, bv = block
        scores = jnp.einsum('thc,shc->hts', bq.astype(jnp.float32), bk.astype(jnp.float32))
        weights = jnp.where(causal, scores, 0.0).astype(jnp.bfloat16)
        intra = jnp.einsum('hts,shc->thc', weights.astype(jnp.float32), bv.astype(jnp.float32))
        inter = jnp.einsum('thc,hcd->thd', bq.astype(jnp.float32), prefix, precision=lax.Precision.HIGHEST)
        mixed = intra + inter
        scale = lax.rsqrt(lax.optimization_barrier(jnp.mean(mixed * mixed, axis=2, keepdims=True)) + 1e-05)
        attn = (mixed * scale * gain[None]).astype(jnp.bfloat16).reshape(TOK_DEV, HEADS * HD)
        total = jnp.zeros((TOK_DEV, D), jnp.float32)
        for index in range(N_HEAD):
            part = jnp.dot(attn[:, index * group:(index + 1) * group], w_out[index * group:(index + 1) * group], preferred_element_type=jnp.float32).astype(jnp.bfloat16)
            part = lax.optimization_barrier(part)
            total = total + part.astype(jnp.float32)
        local = jnp.einsum('thc,thd->hcd', bk.astype(jnp.float32), bv.astype(jnp.float32))
        return (prefix + local, total.astype(jnp.bfloat16))
    start = jnp.zeros((HEADS, HD, HD), jnp.float32)
    _, outputs = lax.scan(step, start, (fq, fk, vals))
    return outputs.reshape(N_CTX * TOK_DEV, D)
```

```python
import functools

import jax
import jax.numpy as jnp
from jax import lax
from jax.experimental import pallas as pl
from jax.experimental.pallas import tpu as pltpu
from jax.sharding import PartitionSpec as P

NZ, NY, NX = 8, 8, 4
HD = 128
TOK = 128
HALF = 512
HEADS = HALF // HD
SL = 64
WB = 32
F32, BF16 = jnp.float32, jnp.bfloat16
NT = (((1,), (1,)), ((), ()))
TN = (((0,), (0,)), ((), ()))


def feature(x):
    x = x.astype(F32)
    return jnp.where(x > 0.0, x + 1.0, jnp.exp(jnp.minimum(x, 0.0))).astype(BF16)


def dot(a, b, dims=(((1,), (0,)), ((), ()))):
    return lax.dot_general(a, b, dims, preferred_element_type=F32)


def kernel(
    q_ref, k_ref, v_ref, g_ref, w_ref, o_ref,
    wa, wb, qx, kx, vx, s_out, s_in, e_buf, r_out, r_in, f_out, pf, mixed, attn,
    p2, ra, rb, p1, pm, fin, p0, sib, tot,
    s_qkv, r_qkv, s_a1, r_a1, s_b1, r_b1, s_a2, r_a2, s_b2, r_b2,
    s_p1, r_p1, s_p2, r_p2, s_p3, r_p3, s_at, r_at, s_x, r_x, s_f, r_f, s_s, r_s,
):
    me = lax.axis_index("ctx")
    x = lax.axis_index("head")
    c = lax.rem(me, 2)
    p = lax.div(me, 2)
    y = lax.rem(p, NY)
    z = lax.div(p, NY)

    def dev(zz, yy, cc, xx):
        return ((zz * NY + yy) * 2 + cc, xx)

    def up(a, d, n):
        return lax.rem(a + d, n)

    def down(a, d, n):
        return lax.rem(a + n - d, n)

    def remote(src, dst, ss, rs, to):
        return pltpu.make_async_remote_copy(
            src_ref=src, dst_ref=dst, send_sem=ss, recv_sem=rs,
            device_id=to, device_id_type=pl.DeviceIdType.MESH,
        )

    here = dev(z, y, c, x)
    sibling = dev(z, y, 1 - c, x)
    x_up, x_dn = up(x, 1, NX), down(x, 1, NX)

    barrier = pltpu.get_barrier_semaphore()

    def greet(to):
        pl.semaphore_signal(barrier, inc=1, device_id=to, device_id_type=pl.DeviceIdType.MESH)

    greet(sibling)

    @pl.loop(1, NY)
    def _(d):
        greet(dev(z, up(y, d, NY), c, x))

    @pl.loop(1, NZ)
    def _(d):
        greet(dev(up(z, d, NZ), y, c, x))

    for xx in (x_up, x_dn):
        for cc in range(2):
            greet(dev(z, y, cc, xx))

    mine = pl.ds(pl.multiple_of(c * TOK, TOK), TOK)
    other = pl.ds(pl.multiple_of((1 - c) * TOK, TOK), TOK)
    cols = pl.ds(pl.multiple_of(c * HALF, HALF), HALF)
    cols_other = pl.ds(pl.multiple_of((1 - c) * HALF, HALF), HALF)
    wa[z, y] = w_ref[:, :HALF]
    wb[z, y] = w_ref[:, HALF:]
    for src, dst in ((k_ref, kx), (v_ref, vx), (q_ref, qx)):
        dst[mine, :] = src[:, cols]

    pl.semaphore_wait(barrier, 1 + (NY - 1) + (NZ - 1) + 4)

    qkv = [
        remote(src.at[:, cols_other], dst.at[mine], s_qkv.at[i], r_qkv.at[i], sibling)
        for i, (src, dst) in enumerate(((k_ref, kx), (v_ref, vx), (q_ref, qx)))
    ]
    qkv_in = [
        remote(src.at[:, cols_other], dst.at[other], s_qkv.at[i], r_qkv.at[i], sibling)
        for i, (src, dst) in enumerate(((k_ref, kx), (v_ref, vx), (q_ref, qx)))
    ]
    for copy in qkv:
        copy.start()

    def a1(zz, yy, d, to):
        ref = wa.at[zz, yy]
        return remote(ref, ref, s_a1.at[d], r_a1.at[d], to)

    def b1(zz, yy, d, to):
        ref = wb.at[zz, yy]
        return remote(ref, ref, s_b1.at[d], r_b1.at[d], to)

    @pl.loop(1, NY)
    def _(d):
        a1(z, y, d, dev(z, up(y, d, NY), c, x)).start()

    @pl.loop(1, NZ)
    def _(d):
        b1(z, y, d, dev(up(z, d, NZ), y, c, x)).start()

    def ring(step, arriving):
        copies = []
        for way in range(2):
            gap = step if arriving else step - 1
            hop_z = dev(up(z, 1, NZ) if way == 0 else down(z, 1, NZ), y, c, x)
            hop_y = dev(z, up(y, 1, NY) if way == 0 else down(y, 1, NY), c, x)
            row = down(z, gap, NZ) if way == 0 else up(z, gap, NZ)
            col = down(y, gap, NY) if way == 0 else up(y, gap, NY)
            for j in range(2):
                if step == NY // 2 and j != way:
                    continue
                i = (way * 4 + step - 1) * 2 + j
                ref_a = wa.at[row, pl.ds(4 * j, 4)]
                ref_b = wb.at[pl.ds(4 * j, 4), col]
                copies.append(remote(ref_a, ref_a, s_a2.at[i], r_a2.at[i], hop_z))
                copies.append(remote(ref_b, ref_b, s_b2.at[i], r_b2.at[i], hop_y))
        return copies

    def ring_send(step):
        for copy in ring(step, False):
            copy.start()

    def ring_recv(step):
        for copy in ring(step, True):
            copy.wait_recv()

    qkv_in[0].wait_recv()
    qkv_in[1].wait_recv()
    fk = feature(kx[...])
    for h in range(HEADS):
        hs = slice(h * HD, (h + 1) * HD)
        state = dot(fk[:, hs], vx[:, hs], TN).astype(BF16)
        s_out[2 * h] = state[:SL]
        s_out[2 * h + 1] = state[SL:]

    def send_1(d, arriving):
        yy = down(y, d, NY) if arriving else up(y, d, NY)
        slot = s_in.at[yy if arriving else y]
        return remote(s_out.at[yy], slot, s_p1.at[d], r_p1.at[d], dev(z, yy, c, x))

    @pl.loop(1, NY)
    def _(d):
        send_1(d, False).start()

    s_in[y] = s_out[y]

    qkv_in[2].wait_recv()
    fq = feature(qx[...])
    rows = lax.broadcasted_iota(jnp.int32, (2 * TOK, 2 * TOK), 0)
    columns = lax.broadcasted_iota(jnp.int32, (2 * TOK, 2 * TOK), 1)
    for h in range(HEADS):
        hs = slice(h * HD, (h + 1) * HD)
        scores = dot(fq[:, hs], fk[:, hs], NT)
        weights = jnp.where(rows >= columns, scores, 0.0).astype(BF16)
        mixed[:, hs] = dot(weights, vx[:, hs])

    @pl.loop(1, NY)
    def _(d):
        a1(z, down(y, d, NY), d, here).wait_recv()

    @pl.loop(1, NZ)
    def _(d):
        b1(down(z, d, NZ), y, d, here).wait_recv()

    ring_send(1)

    @pl.loop(1, NY)
    def _(d):
        send_1(d, True).wait_recv()

    run = jnp.zeros((SL, HD), F32)
    for i in range(NY):
        e_buf[i] = run
        run = run + s_in[i].astype(F32)
    r_out[...] = run.astype(BF16)

    def send_2(d, arriving):
        zz = down(z, d, NZ) if arriving else up(z, d, NZ)
        slot = r_in.at[zz if arriving else z]
        return remote(r_out, slot, s_p2.at[d], r_p2.at[d], dev(zz, y, c, x))

    @pl.loop(1, NZ)
    def _(d):
        send_2(d, False).start()

    r_in[z] = r_out[...]

    ring_recv(1)
    ring_send(2)

    @pl.loop(1, NZ)
    def _(d):
        send_2(d, True).wait_recv()

    before = jnp.zeros((SL, HD), F32)
    for i in range(NZ):
        before = before + jnp.where(i < z, r_in[i].astype(F32), 0.0)
    for i in range(NY):
        f_out[i] = (before + e_buf[i]).astype(BF16)

    def send_3(d, arriving):
        yy = down(y, d, NY) if arriving else up(y, d, NY)
        slot = pf.at[yy if arriving else y]
        return remote(f_out.at[yy], slot, s_p3.at[d], r_p3.at[d], dev(z, yy, c, x))

    @pl.loop(1, NY)
    def _(d):
        send_3(d, False).start()

    pf[y] = f_out[y]

    ring_recv(2)
    ring_send(3)

    @pl.loop(1, NY)
    def _(d):
        send_3(d, True).wait_recv()

    def at_copy(h, who):
        ref = attn.at[:, pl.ds(pl.multiple_of(who * HALF + h * HD, HD), HD)]
        return remote(ref, ref, s_at.at[h], r_at.at[h], sibling)

    for h in range(HEADS):
        hs = slice(h * HD, (h + 1) * HD)
        at = pl.ds(pl.multiple_of(c * HALF + h * HD, HD), HD)
        prefix = pf[2 * h : 2 * h + 2].reshape(HD, HD)
        total = mixed[:, hs] + dot(fq[:, hs], prefix)
        scale = lax.rsqrt(jnp.mean(total * total, axis=1, keepdims=True) + 1e-05)
        attn[:, at] = (total * scale * g_ref[:, at]).astype(BF16)
        at_copy(h, c).start()

    ring_recv(3)
    ring_send(4)
    for h in range(HEADS):
        at_copy(h, 1 - c).wait_recv()
    ring_recv(4)

    def share(xx, tokens):
        w_a = wa[pl.ds(2 * xx, 2)].reshape(HALF, HALF)
        w_b = wb[pl.ds(2 * xx, 2)].reshape(HALF, HALF)
        return dot(attn[tokens, :HALF], w_a, NT) + dot(attn[tokens, HALF:], w_b, NT)

    lo, hi = pl.ds(0, TOK), pl.ds(TOK, TOK)
    x_far = up(x, 2, NX)
    far_up = remote(p2.at[0], ra, s_x.at[0], r_x.at[0], dev(z, y, c, x_up))
    far_dn = remote(p2.at[1], rb, s_x.at[1], r_x.at[1], dev(z, y, c, x_dn))
    near_up = [
        remote(p1.at[i], fin.at[c, 0], s_f.at[i], r_f.at[2 * c], dev(z, y, i, x_up)) for i in range(2)
    ]
    near_dn = [
        remote(pm.at[i], fin.at[c, 1], s_f.at[2 + i], r_f.at[2 * c + 1], dev(z, y, i, x_dn))
        for i in range(2)
    ]
    p2[0] = share(x_far, lo).astype(BF16)
    far_up.start()
    p2[1] = share(x_far, hi).astype(BF16)
    far_dn.start()
    p1[1] = share(x_up, hi).astype(BF16)
    near_up[1].start()
    pm[0] = share(x_dn, lo).astype(BF16)
    near_dn[0].start()
    part_up = share(x_up, lo)
    far_up.wait_recv()
    p1[0] = (part_up + ra[...].astype(F32)).astype(BF16)
    near_up[0].start()
    part_dn = share(x_dn, hi)
    far_dn.wait_recv()
    pm[1] = (part_dn + rb[...].astype(F32)).astype(BF16)
    near_dn[1].start()
    p0[...] = share(x, other).astype(BF16)
    across = remote(p0, sib, s_s, r_s, sibling)
    across.start()
    own = share(x, mine)

    for i in range(4):
        remote(fin.at[i // 2, i % 2], fin.at[i // 2, i % 2], s_f.at[i], r_f.at[i], here).wait_recv()
    across.wait_recv()
    tot[c] = own + fin[c, 0].astype(F32) + fin[c, 1].astype(F32)
    tot[1 - c] = sib[...].astype(F32) + fin[1 - c, 0].astype(F32) + fin[1 - c, 1].astype(F32)

    run_of = lax.div(lax.broadcasted_iota(jnp.int32, (TOK, HD), 1), WB)
    for j in range(HALF // HD):
        a = tot[0, :, j * HD : (j + 1) * HD]
        b = tot[1, :, j * HD : (j + 1) * HD]
        a_r, b_r = pltpu.roll(a, 32, 1), pltpu.roll(b, 32, 1)
        a_l, b_l = pltpu.roll(a, 96, 1), pltpu.roll(b, 96, 1)
        a_h, b_h = pltpu.roll(a, 64, 1), pltpu.roll(b, 64, 1)

        def pick(t0, t1, t2, t3):
            low = jnp.where(run_of == 0, t0, t1)
            high = jnp.where(run_of == 2, t2, t3)
            return jnp.where(run_of < 2, low, high).astype(BF16)

        o_ref[:, 2 * j * HD : (2 * j + 1) * HD] = pick(a, b_r, a_r, b_h)
        o_ref[:, (2 * j + 1) * HD : (2 * j + 2) * HD] = pick(a_h, b_l, a_l, b)

    for copy in qkv:
        copy.wait_send()

    @pl.loop(1, NY)
    def _(d):
        a1(z, y, d, here).wait_send()
        b1(z, y, d, here).wait_send()
        send_1(d, False).wait_send()
        send_2(d, False).wait_send()
        send_3(d, False).wait_send()

    for step in range(1, 5):
        for copy in ring(step, False):
            copy.wait_send()
    for h in range(HEADS):
        at_copy(h, c).wait_send()
    for copy in (far_up, far_dn, *near_up, *near_dn, across):
        copy.wait_send()


def per_device(queries, keys, values, head_gain, w_out):
    dma = pltpu.SemaphoreType.DMA
    vmem = pltpu.VMEM
    scratch = [
        vmem((NZ, NY, WB, HALF), BF16),
        vmem((NZ, NY, WB, HALF), BF16),
        vmem((2 * TOK, HALF), BF16),
        vmem((2 * TOK, HALF), BF16),
        vmem((2 * TOK, HALF), BF16),
        vmem((NY, SL, HD), BF16),
        vmem((NY, SL, HD), BF16),
        vmem((NY, SL, HD), F32),
        vmem((SL, HD), BF16),
        vmem((NZ, SL, HD), BF16),
        vmem((NY, SL, HD), BF16),
        vmem((NY, SL, HD), BF16),
        vmem((2 * TOK, HALF), F32),
        vmem((2 * TOK, 2 * HALF), BF16),
        vmem((2, TOK, HALF), BF16),
        vmem((TOK, HALF), BF16),
        vmem((TOK, HALF), BF16),
        vmem((2, TOK, HALF), BF16),
        vmem((2, TOK, HALF), BF16),
        vmem((2, 2, TOK, HALF), BF16),
        vmem((TOK, HALF), BF16),
        vmem((TOK, HALF), BF16),
        vmem((2, TOK, HALF), F32),
        dma((3,)), dma((3,)),
        dma((8,)), dma((8,)), dma((8,)), dma((8,)),
        dma((16,)), dma((16,)), dma((16,)), dma((16,)),
        dma((8,)), dma((8,)), dma((8,)), dma((8,)), dma((8,)), dma((8,)),
        dma((HEADS,)), dma((HEADS,)),
        dma((2,)), dma((2,)),
        dma((4,)), dma((4,)),
        dma(()), dma(()),
    ]
    whole = pl.BlockSpec(memory_space=pltpu.VMEM)
    return pl.pallas_call(
        kernel,
        out_shape=jax.ShapeDtypeStruct(queries.shape, BF16),
        in_specs=[whole] * 5,
        out_specs=whole,
        scratch_shapes=scratch,
        compiler_params=pltpu.CompilerParams(
            collective_id=0, has_side_effects=True, vmem_limit_bytes=40 * 2**20
        ),
        cost_estimate=pl.CostEstimate(flops=2**31, bytes_accessed=2**21, transcendentals=2**19),
    )(queries, keys, values, head_gain.reshape(1, -1), w_out.T)


def solution(mesh):
    placed = (P("ctx", "head"), P("ctx", "head"), P("ctx", "head"), P("head"), P("head", "ctx"))
    return jax.shard_map(
        per_device, mesh=mesh, in_specs=placed, out_specs=P("ctx", "head"), check_vma=False
    )
```

```python
import jax
import jax.numpy as jnp
from jax import lax
from jax.experimental import pallas as pl
from jax.experimental.pallas import tpu as pltpu
from jax.sharding import PartitionSpec as P

NZ, NY, NX = 8, 8, 4
HD = 128
TOK = 128
HALF = 512
HEADS = HALF // HD
SL = 64
WB = 16
GROUPS = ((0, 1), (1, 2), (3, 2), (5, 2), (7, 1))
LAST = (((0, 1, 2), (3, 4)), ((3, 4), (0, 1, 2)))
ORDER = (0, 1, -1, 2, -2, 3, -3, 4)
FAR_FIRST = (4, 3, 5, 2, 6, 1, 7)
F32, BF16 = jnp.float32, jnp.bfloat16


def slot_of(rel):
    return 2 * rel - 1 if rel > 0 else -2 * rel


def feature(x):
    x = x.astype(F32)
    return jnp.where(x > 0.0, x + 1.0, jnp.exp(jnp.minimum(x, 0.0))).astype(BF16)


def dot(a, b):
    return jnp.dot(a, b, preferred_element_type=F32)


def up(a, d, n):
    return lax.rem(a + d, n)


def down(a, d, n):
    return lax.rem(a + n - d, n)


def kernel(
    q_ref, k_ref, v_ref, g_ref, w_ref, o_ref,
    gain, wa, wb, qx, kx, vx, s_out, s_in, e_buf, r_out, r_in, f_out, pf, mixed, attn,
    near, got, fin, sib, part, out_t,
    s_in0, s_qkv, r_qkv, s_line, r_line, s_ring, r_ring,
    s_p1, r_p1, s_p2, r_p2, s_p3, r_p3, s_at, r_at, s_far, r_far, s_near, r_fin, r_sib,
):
    me = lax.axis_index("ctx")
    x = lax.axis_index("head")
    c = lax.rem(me, 2)
    p = lax.div(me, 2)
    y = lax.rem(p, NY)
    z = lax.div(p, NY)

    def dev(zz, yy, cc, xx):
        return ((zz * NY + yy) * 2 + cc, xx)

    def remote(src, dst, ss, rs, to):
        return pltpu.make_async_remote_copy(
            src_ref=src, dst_ref=dst, send_sem=ss, recv_sem=rs,
            device_id=to, device_id_type=pl.DeviceIdType.MESH,
        )

    sibling = dev(z, y, 1 - c, x)
    x_up, x_dn = up(x, 1, NX), down(x, 1, NX)

    mine = pl.ds(pl.multiple_of(c * TOK, TOK), TOK)
    other = pl.ds(pl.multiple_of((1 - c) * TOK, TOK), TOK)
    cols = pl.ds(pl.multiple_of(c * HALF, HALF), HALF)
    cols_other = pl.ds(pl.multiple_of((1 - c) * HALF, HALF), HALF)
    qkv_refs = ((k_ref, kx), (v_ref, vx), (q_ref, qx))
    inputs = [
        pltpu.make_async_copy(w_ref.at[pl.ds(0, WB)], wa.at[z, 0], s_in0.at[0]),
        pltpu.make_async_copy(w_ref.at[pl.ds(WB, WB)], wb.at[y, 0], s_in0.at[1]),
    ]
    for i, (src, dst) in enumerate(qkv_refs):
        inputs.append(pltpu.make_async_copy(src.at[:, cols], dst.at[mine], s_in0.at[2 + i]))
    inputs.append(pltpu.make_async_copy(g_ref, gain, s_in0.at[5]))
    for copy in inputs:
        copy.start()

    barrier = pltpu.get_barrier_semaphore()

    def greet(to):
        pl.semaphore_signal(barrier, inc=1, device_id=to, device_id_type=pl.DeviceIdType.MESH)

    greet(sibling)

    @pl.loop(1, NY)
    def _(d):
        greet(dev(z, up(y, d, NY), c, x))

    @pl.loop(1, NZ)
    def _(d):
        greet(dev(up(z, d, NZ), y, c, x))

    for xx in (x_up, x_dn):
        for cc in range(2):
            greet(dev(z, y, cc, xx))

    def at_y(yy):
        return dev(z, yy, c, x)

    def at_z(zz):
        return dev(zz, y, c, x)

    kinds = ((wa, y, z, at_y, at_z), (wb, z, y, at_z, at_y))

    def line(kind, way, k, arriving):
        buf, u, t, at_u, _ = kinds[kind]
        sign = 1 if way else -1
        rel = 4 if k == 4 else sign * k
        dst = buf.at[t, slot_of(rel)]
        hop = (1, 2, 1, 2)[k - 1]
        src = dst if arriving else buf.at[t, slot_of(sign * (k - hop))]
        if not arriving and k < 3:
            src = w_ref.at[pl.ds(kind * WB, WB)]
        i = (kind * 2 + way) * 4 + k - 1
        to = at_u(down(u, hop, NY) if way else up(u, hop, NY))
        return remote(src, dst, s_line.at[i], r_line.at[i], to)

    def ring(kind, way, step, group, arriving):
        buf, _, t, _, at_t = kinds[kind]
        gap = step if arriving else step - 1
        row = up(t, gap, NZ) if way else down(t, gap, NZ)
        ref = buf.at[row, pl.ds(*GROUPS[group])]
        src = ref
        if step == 1 and group == 0 and not arriving:
            ref = buf.at[row, 0]
            src = w_ref.at[pl.ds(kind * WB, WB)]
        i = ((kind * 2 + way) * 4 + step - 1) * 5 + group
        to = at_t(down(t, 1, NZ) if way else up(t, 1, NZ))
        return remote(src, ref, s_ring.at[i], r_ring.at[i], to)

    both = [(kind, way) for kind in range(2) for way in range(2)]

    def ring_send(step, group):
        for kind, way in both:
            if step < 4 or group in LAST[kind][way]:
                ring(kind, way, step, group, False).start()

    def ring_recv(step, group):
        for kind, way in both:
            if step < 4 or group in LAST[kind][way]:
                ring(kind, way, step, group, True).wait_recv()
                if step < 3 or (step == 3 and group in LAST[kind][way]):
                    ring(kind, way, step + 1, group, False).start()

    def line_send(k):
        for kind, way in both:
            if k < 4 or kind == way:
                line(kind, way, k, False).start()

    def line_recv(k):
        for kind, way in both:
            if k < 4 or kind == way:
                line(kind, way, k, True).wait_recv()

    pl.semaphore_wait(barrier, 1 + (NY - 1) + (NZ - 1) + 4)

    qkv = [
        remote(src.at[:, cols_other], dst.at[mine], s_qkv.at[i], r_qkv.at[i], sibling)
        for i, (src, dst) in enumerate(qkv_refs)
    ]
    qkv_in = [
        remote(src.at[:, cols_other], dst.at[other], s_qkv.at[i], r_qkv.at[i], sibling)
        for i, (src, dst) in enumerate(qkv_refs)
    ]
    for copy in qkv:
        copy.start()
    ring_send(1, 0)
    line_send(1)
    line_send(2)

    def send_1(d, arriving):
        yy = down(y, d, NY) if arriving else up(y, d, NY)
        slot = s_in.at[yy if arriving else y]
        return remote(s_out.at[yy], slot, s_p1.at[d], r_p1.at[d], dev(z, yy, c, x))

    def send_2(d, arriving):
        zz = down(z, d, NZ) if arriving else up(z, d, NZ)
        slot = r_in.at[zz if arriving else z]
        return remote(r_out, slot, s_p2.at[d], r_p2.at[d], dev(zz, y, c, x))

    def send_3(d, arriving):
        yy = down(y, d, NY) if arriving else up(y, d, NY)
        slot = pf.at[yy if arriving else y]
        return remote(f_out.at[yy], slot, s_p3.at[d], r_p3.at[d], dev(z, yy, c, x))

    def at_copy(h, who):
        ref = attn.at[pl.ds(pl.multiple_of(who * HALF + h * HD, HD), HD)]
        return remote(ref, ref, s_at.at[h], r_at.at[h], sibling)

    held = {}

    def states():
        for copy in inputs:
            copy.wait()
        qkv_in[0].wait_recv()
        held['fk'] = fk = feature(kx[...])
        qkv_in[1].wait_recv()
        held['v_t'] = v_t = vx[...].T
        for h in range(HEADS):
            hs = slice(h * HD, (h + 1) * HD)
            state = dot(v_t[hs], fk[:, hs]).astype(BF16)
            s_out[2 * h] = state[:SL]
            s_out[2 * h + 1] = state[SL:]

        for d in FAR_FIRST:
            send_1(d, False).start()

        s_in[y] = s_out[y]

    def inside():
        qkv_in[2].wait_recv()
        fk, v_t = held['fk'], held['v_t']
        held['fq_t'] = fq_t = feature(qx[...]).T
        keys_at = lax.broadcasted_iota(jnp.int32, (2 * TOK, 2 * TOK), 0)
        query_at = lax.broadcasted_iota(jnp.int32, (2 * TOK, 2 * TOK), 1)
        for h in range(HEADS):
            hs = slice(h * HD, (h + 1) * HD)
            scores = dot(fk[:, hs], fq_t[hs])
            weights = jnp.where(keys_at <= query_at, scores, 0.0).astype(BF16)
            mixed[hs] = dot(v_t[hs], weights)

    def row_prefix():
        for d in FAR_FIRST:
            send_1(d, True).wait_recv()

        run = jnp.zeros((SL, HD), F32)
        for i in range(NY):
            e_buf[i] = run
            run = run + s_in[i].astype(F32)
        r_out[...] = run.astype(BF16)

        for d in FAR_FIRST:

            @pl.when(z + d < NZ)
            def _():
                send_2(d, False).start()

        r_in[z] = r_out[...]

    def all_prefix():
        for d in FAR_FIRST:

            @pl.when(z >= d)
            def _():
                send_2(d, True).wait_recv()

        before = jnp.zeros((SL, HD), F32)
        for i in range(NZ):
            before = before + jnp.where(i < z, r_in[i].astype(F32), 0.0)
        for i in range(NY):
            f_out[i] = (before + e_buf[i]).astype(BF16)

        for d in FAR_FIRST:
            send_3(d, False).start()

        pf[y] = f_out[y]

    def attend():
        fq_t = held['fq_t']
        gains = []
        for h in range(HEADS):
            at = pl.ds(pl.multiple_of(c * HALF + h * HD, HD), HD)
            turned = jnp.broadcast_to(gain[:, at], (HD, HD)).T
            gains.append(jnp.concatenate([turned, turned], axis=1))

        for d in FAR_FIRST:
            send_3(d, True).wait_recv()

        for h in range(HEADS):
            hs = slice(h * HD, (h + 1) * HD)
            at = pl.ds(pl.multiple_of(c * HALF + h * HD, HD), HD)
            prefix = pf[2 * h : 2 * h + 2].reshape(HD, HD)
            total = mixed[hs] + dot(prefix, fq_t[hs])
            scale = lax.rsqrt(jnp.mean(total * total, axis=0, keepdims=True) + 1e-05)
            attn[at] = (total * scale * gains[h]).astype(BF16)
            at_copy(h, c).start()

    def unit_a(i):
        zz = up(z, jnp.where(lax.rem(i, 2) == 1, lax.div(i + 1, 2), NZ - lax.div(i, 2)), NZ)
        return zz, lax.div(zz, 2), 0, lax.rem(zz, 2), lambda: wa[zz].reshape(NY * WB, 2 * HALF)

    def unit_b(rel, grp):
        xx = up(x, rel, NX)

        def blocks():
            found = []
            for zl in range(2):
                d = up(2 * xx + zl, NZ - z, NZ)
                slot = jnp.where(d <= 4, jnp.maximum(2 * d - 1, 0), 2 * NZ - 2 * d)
                for off in ORDER[4 * grp : 4 * grp + 4]:
                    found.append(wb[up(y, off % NY, NY), slot])
            return jnp.concatenate(found, axis=0)

        return NZ + 2 * xx + grp, xx, 1, grp, blocks

    def far_copy(n, i):
        rows = pl.ds(i * SL, SL)
        to = dev(z, y, c, x_dn if i else x_up)
        return remote(near.at[n, :, rows], got.at[n, i], s_far.at[n, i], r_far.at[n, i], to)

    def near_copy(n, kind, idx, way, core):
        to = dev(z, y, core, jnp.where(way == 0, x_up, x_dn))
        return remote(
            near.at[n, core], fin.at[c, kind, idx, way], s_near.at[n, core],
            r_fin.at[((c * 2 + kind) * 2 + idx) * 2 + way], to,
        )

    def sib_copy(n, kind, idx):
        i = kind * 2 + idx
        return remote(near.at[n, 1 - c], sib.at[i], s_near.at[n, 0], r_sib.at[i], sibling)

    def far_unit(n, xx, kind, idx, blocks):
        @pl.when(up(xx, NX - x, NX) == 2)
        def _():
            total = dot(blocks(), attn[...]).astype(BF16)
            for core in range(2):
                near[n, core] = total[:, core * TOK : (core + 1) * TOK]
            for i in range(2):
                far_copy(n, i).start()

    def near_unit(n, xx, kind, idx, blocks):
        rel = up(xx, NX - x, NX)

        @pl.when(lax.rem(rel, 2) == 1)
        def _():
            total = dot(blocks(), attn[...])
            way = lax.div(rel, 2)
            rows = pl.ds(pl.multiple_of(way * SL, SL), SL)
            for core in range(2):
                part[core] = total[:, core * TOK : (core + 1) * TOK]
                near[n, core] = part[core].astype(BF16)
            far_copy_in = remote(got.at[n, way], got.at[n, way], s_far.at[n, way], r_far.at[n, way], sibling)
            far_copy_in.wait_recv()
            for core in range(2):
                near[n, core, rows] = (part[core, rows] + got[n, way, core].astype(F32)).astype(BF16)
                near_copy(n, kind, idx, way, core).start()

        @pl.when(rel == 0)
        def _():
            total = dot(blocks(), attn[...]).astype(BF16)
            for core in range(2):
                near[n, core] = total[:, core * TOK : (core + 1) * TOK]
            sib_copy(n, kind, idx).start()

    def far_units(first, last, grp):
        @pl.loop(first, last)
        def _(i):
            far_unit(*unit_a(i))

        far_unit(*unit_b(2, grp))

    def near_units(first, last, grp):
        @pl.loop(first, last)
        def _(i):
            near_unit(*unit_a(i))

        for rel in (1, 3, 0):
            near_unit(*unit_b(rel, grp))

    def line_1():
        line_recv(1)
        ring_send(1, 1)

    def line_2():
        line_recv(2)
        line_send(3)
        line_send(4)
        ring_send(1, 2)

    def line_3():
        line_recv(3)
        ring_send(1, 3)
        line_recv(4)
        ring_send(1, 4)

    def swap():
        for h in range(HEADS):
            at_copy(h, 1 - c).wait_recv()

    def early_far():
        far_units(0, 5, 0)

    def early_near():
        near_units(0, 5, 0)

    def late_far():
        far_units(5, NZ, 1)

    def late_near():
        near_units(5, NZ, 1)

    def rings(*pairs):
        for pair in pairs:
            ring_recv(*pair)

    states()
    line_1()
    line_2()
    inside()
    line_3()
    rings((1, 1), (1, 2))
    row_prefix()
    rings((1, 3), (1, 4), (1, 0), (2, 1))
    all_prefix()
    rings((2, 2), (2, 3), (2, 4), (2, 0))
    attend()
    rings((3, 1), (3, 2), (3, 3), (3, 4), (3, 0))
    swap()
    early_far()
    rings((4, 0), (4, 1), (4, 2), (4, 3), (4, 4))
    late_far()
    early_near()
    late_near()
    for i in range(16):
        ref = fin.at[i // 8, (i // 4) % 2, (i // 2) % 2, i % 2]
        remote(ref, ref, s_near.at[0, 0], r_fin.at[i], sibling).wait_recv()
    for i in range(4):
        remote(sib.at[i], sib.at[i], s_near.at[0, 0], r_sib.at[i], sibling).wait_recv()

    for s in range(2):
        for kind in range(2):
            for idx in range(2):
                n = 2 * x + idx + kind * NZ
                own = jnp.where(s == c, near[n, c].astype(F32), sib[kind * 2 + idx].astype(F32))
                total = own + fin[s, kind, idx, 0].astype(F32) + fin[s, kind, idx, 1].astype(F32)
                for i in range(NY):
                    zl, off = (idx, ORDER[i]) if kind == 0 else (i // 4, ORDER[4 * idx + i % 4])
                    out_t[zl * NY + up(y, off % NY, NY), 2 * s + kind] = total[i * WB : (i + 1) * WB]
    for j in range(NY):
        o_ref[:, j * HD : (j + 1) * HD] = out_t[2 * j : 2 * j + 2].reshape(HD, HD).T.astype(BF16)

    for copy in qkv:
        copy.wait_send()

    @pl.loop(1, NY)
    def _(d):
        send_1(d, False).wait_send()
        send_3(d, False).wait_send()

        @pl.when(z + d < NZ)
        def _():
            send_2(d, False).wait_send()

    for kind, way in both:
        for k in range(1, 5):
            if k < 4 or kind == way:
                line(kind, way, k, False).wait_send()
        for step in range(1, 5):
            for group in range(5):
                if step < 4 or group in LAST[kind][way]:
                    ring(kind, way, step, group, False).wait_send()
    for h in range(HEADS):
        at_copy(h, c).wait_send()

    def unit_left(n, xx, kind, idx, blocks):
        rel = up(xx, NX - x, NX)

        @pl.when(rel == 2)
        def _():
            for i in range(2):
                far_copy(n, i).wait_send()

        @pl.when(lax.rem(rel, 2) == 1)
        def _():
            for core in range(2):
                near_copy(n, kind, idx, lax.div(rel, 2), core).wait_send()

        @pl.when(rel == 0)
        def _():
            sib_copy(n, kind, idx).wait_send()

    @pl.loop(0, NZ)
    def _(i):
        unit_left(*unit_a(i))

    for rel in range(NX):
        for grp in range(2):
            unit_left(*unit_b(rel, grp))


def per_device(queries, keys, values, head_gain, w_out):
    dma = pltpu.SemaphoreType.DMA
    vmem = pltpu.VMEM
    rows = NY * WB
    scratch = [
        vmem((1, 2 * HALF), F32),
        vmem((NZ, NY, WB, 2 * HALF), BF16),
        vmem((NY, NZ, WB, 2 * HALF), BF16),
        vmem((2 * TOK, HALF), BF16),
        vmem((2 * TOK, HALF), BF16),
        vmem((2 * TOK, HALF), BF16),
        vmem((NY, SL, HD), BF16),
        vmem((NY, SL, HD), BF16),
        vmem((NY, SL, HD), F32),
        vmem((SL, HD), BF16),
        vmem((NZ, SL, HD), BF16),
        vmem((NY, SL, HD), BF16),
        vmem((NY, SL, HD), BF16),
        vmem((HALF, 2 * TOK), F32),
        vmem((2 * HALF, 2 * TOK), BF16),
        vmem((16, 2, rows, TOK), BF16),
        vmem((16, 2, 2, SL, TOK), BF16),
        vmem((2, 2, 2, 2, rows, TOK), BF16),
        vmem((4, rows, TOK), BF16),
        vmem((2, rows, TOK), F32),
        vmem((2 * NY, 4, WB, TOK), F32),
        dma((6,)),
        dma((3,)), dma((3,)),
        dma((16,)), dma((16,)), dma((80,)), dma((80,)),
        dma((8,)), dma((8,)), dma((8,)), dma((8,)), dma((8,)), dma((8,)),
        dma((HEADS,)), dma((HEADS,)),
        dma((16, 2)), dma((16, 2)), dma((16, 2)),
        dma((16,)), dma((4,)),
    ]
    return pl.pallas_call(
        kernel,
        out_shape=jax.ShapeDtypeStruct(queries.shape, BF16),
        in_specs=[pl.BlockSpec(memory_space=pl.ANY)] * 5,
        out_specs=pl.BlockSpec(memory_space=pltpu.VMEM),
        scratch_shapes=scratch,
        compiler_params=pltpu.CompilerParams(
            collective_id=0, has_side_effects=True, vmem_limit_bytes=60 * 2**20
        ),
        cost_estimate=pl.CostEstimate(flops=2**31, bytes_accessed=2**21, transcendentals=2**19),
    )(queries, keys, values, head_gain.reshape(1, -1), w_out.T)


def solution(mesh):
    placed = (P("ctx", "head"), P("ctx", "head"), P("ctx", "head"), P("head"), P("head", "ctx"))
    return jax.shard_map(
        per_device, mesh=mesh, in_specs=placed, out_specs=P("ctx", "head"), check_vma=False
    )
```

```python
import jax
import jax.numpy as jnp
from jax import lax
from jax.experimental import pallas as pl
from jax.experimental.pallas import tpu as pltpu
from jax.sharding import PartitionSpec as P

NZ, NY, NX = 8, 8, 4
HD = 128
TOK = 128
HALF = 512
HEADS = HALF // HD
SL = 64
WB = 16
GROUPS = ((0, 1), (1, 2), (3, 2), (5, 2), (7, 1))
LAST = (((0, 1, 2), (3, 4)), ((3, 4), (0, 1, 2)))
ORDER = (0, 1, -1, 2, -2, 3, -3, 4)
FAR_FIRST = (4, 3, 5, 2, 6, 1, 7)
F32, BF16 = jnp.float32, jnp.bfloat16


def slot_of(rel):
    return 2 * rel - 1 if rel > 0 else -2 * rel


def feature(x):
    x = x.astype(F32)
    return jnp.where(x > 0.0, x + 1.0, jnp.exp(jnp.minimum(x, 0.0))).astype(BF16)


def dot(a, b):
    return jnp.dot(a, b, preferred_element_type=F32)


def up(a, d, n):
    return lax.rem(a + d, n)


def down(a, d, n):
    return lax.rem(a + n - d, n)


def kernel(
    q_ref, k_ref, v_ref, g_ref, w_ref, o_ref,
    gain, wa, wb, qx, kx, vx, s_out, s_in, e_buf, r_out, r_in, f_out, pf, mixed, attn,
    near, got, fin, sib, part, out_t,
    s_in0, s_qkv, r_qkv, s_line, r_line, s_ring, r_ring,
    s_p1, r_p1, s_p2, r_p2, s_p3, r_p3, s_at, r_at, s_far, r_far, s_near, r_fin, r_sib,
):
    me = lax.axis_index("ctx")
    x = lax.axis_index("head")
    c = lax.rem(me, 2)
    p = lax.div(me, 2)
    y = lax.rem(p, NY)
    z = lax.div(p, NY)

    def dev(zz, yy, cc, xx):
        return ((zz * NY + yy) * 2 + cc, xx)

    def remote(src, dst, ss, rs, to):
        return pltpu.make_async_remote_copy(
            src_ref=src, dst_ref=dst, send_sem=ss, recv_sem=rs,
            device_id=to, device_id_type=pl.DeviceIdType.MESH,
        )

    sibling = dev(z, y, 1 - c, x)
    x_up, x_dn = up(x, 1, NX), down(x, 1, NX)

    mine = pl.ds(pl.multiple_of(c * TOK, TOK), TOK)
    other = pl.ds(pl.multiple_of((1 - c) * TOK, TOK), TOK)
    cols = pl.ds(pl.multiple_of(c * HALF, HALF), HALF)
    cols_other = pl.ds(pl.multiple_of((1 - c) * HALF, HALF), HALF)
    qkv_refs = ((k_ref, kx), (v_ref, vx), (q_ref, qx))
    inputs = [
        pltpu.make_async_copy(w_ref.at[pl.ds(0, WB)], wa.at[z, 0], s_in0.at[0]),
        pltpu.make_async_copy(w_ref.at[pl.ds(WB, WB)], wb.at[y, 0], s_in0.at[1]),
    ]
    for i, (src, dst) in enumerate(qkv_refs):
        inputs.append(pltpu.make_async_copy(src.at[:, cols], dst.at[mine], s_in0.at[2 + i]))
    inputs.append(pltpu.make_async_copy(g_ref, gain, s_in0.at[5]))
    for copy in inputs:
        copy.start()

    barrier = pltpu.get_barrier_semaphore()

    def greet(to):
        pl.semaphore_signal(barrier, inc=1, device_id=to, device_id_type=pl.DeviceIdType.MESH)

    greet(sibling)

    @pl.loop(1, NY)
    def _(d):
        greet(dev(z, up(y, d, NY), c, x))

    @pl.loop(1, NZ)
    def _(d):
        greet(dev(up(z, d, NZ), y, c, x))

    for xx in (x_up, x_dn):
        for cc in range(2):
            greet(dev(z, y, cc, xx))

    def at_y(yy):
        return dev(z, yy, c, x)

    def at_z(zz):
        return dev(zz, y, c, x)

    kinds = ((wa, y, z, at_y, at_z), (wb, z, y, at_z, at_y))

    def line(kind, way, k, arriving):
        buf, u, t, at_u, _ = kinds[kind]
        sign = 1 if way else -1
        rel = 4 if k == 4 else sign * k
        dst = buf.at[t, slot_of(rel)]
        hop = (1, 2, 1, 2)[k - 1]
        src = dst if arriving else buf.at[t, slot_of(sign * (k - hop))]
        if not arriving and k < 3:
            src = w_ref.at[pl.ds(kind * WB, WB)]
        i = (kind * 2 + way) * 4 + k - 1
        to = at_u(down(u, hop, NY) if way else up(u, hop, NY))
        return remote(src, dst, s_line.at[i], r_line.at[i], to)

    def ring(kind, way, step, group, arriving):
        buf, _, t, _, at_t = kinds[kind]
        gap = step if arriving else step - 1
        row = up(t, gap, NZ) if way else down(t, gap, NZ)
        ref = buf.at[row, pl.ds(*GROUPS[group])]
        src = ref
        if step == 1 and group == 0 and not arriving:
            ref = buf.at[row, 0]
            src = w_ref.at[pl.ds(kind * WB, WB)]
        i = ((kind * 2 + way) * 4 + step - 1) * 5 + group
        to = at_t(down(t, 1, NZ) if way else up(t, 1, NZ))
        return remote(src, ref, s_ring.at[i], r_ring.at[i], to)

    both = [(kind, way) for kind in range(2) for way in range(2)]

    def ring_send(step, group):
        for kind, way in both:
            if step < 4 or group in LAST[kind][way]:
                ring(kind, way, step, group, False).start()

    def ring_recv(step, group):
        for kind, way in both:
            if step < 4 or group in LAST[kind][way]:
                ring(kind, way, step, group, True).wait_recv()
                if step < 3 or (step == 3 and group in LAST[kind][way]):
                    ring(kind, way, step + 1, group, False).start()

    def line_send(k):
        for kind, way in both:
            if k < 4 or kind == way:
                line(kind, way, k, False).start()

    def line_recv(k):
        for kind, way in both:
            if k < 4 or kind == way:
                line(kind, way, k, True).wait_recv()

    pl.semaphore_wait(barrier, 1 + (NY - 1) + (NZ - 1) + 4)

    qkv = [
        remote(src.at[:, cols_other], dst.at[mine], s_qkv.at[i], r_qkv.at[i], sibling)
        for i, (src, dst) in enumerate(qkv_refs)
    ]
    qkv_in = [
        remote(src.at[:, cols_other], dst.at[other], s_qkv.at[i], r_qkv.at[i], sibling)
        for i, (src, dst) in enumerate(qkv_refs)
    ]
    for copy in qkv:
        copy.start()
    ring_send(1, 0)
    line_send(1)
    line_send(2)

    def send_1(d, arriving):
        yy = down(y, d, NY) if arriving else up(y, d, NY)
        slot = s_in.at[yy if arriving else y]
        return remote(s_out.at[yy], slot, s_p1.at[d], r_p1.at[d], dev(z, yy, c, x))

    def send_2(d, arriving):
        zz = down(z, d, NZ) if arriving else up(z, d, NZ)
        slot = r_in.at[zz if arriving else z]
        return remote(r_out, slot, s_p2.at[d], r_p2.at[d], dev(zz, y, c, x))

    def send_3(d, arriving):
        yy = down(y, d, NY) if arriving else up(y, d, NY)
        slot = pf.at[yy if arriving else y]
        return remote(f_out.at[yy], slot, s_p3.at[d], r_p3.at[d], dev(z, yy, c, x))

    def at_copy(h, who):
        ref = attn.at[pl.ds(pl.multiple_of(who * HALF + h * HD, HD), HD)]
        return remote(ref, ref, s_at.at[h], r_at.at[h], sibling)

    held = {}

    def states():
        for copy in inputs:
            copy.wait()
        qkv_in[0].wait_recv()
        held['fk'] = fk = feature(kx[...])
        qkv_in[1].wait_recv()
        held['v_t'] = v_t = vx[...].T
        for h in range(HEADS):
            hs = slice(h * HD, (h + 1) * HD)
            state = dot(v_t[hs], fk[:, hs]).astype(BF16)
            s_out[2 * h] = state[:SL]
            s_out[2 * h + 1] = state[SL:]

        for d in FAR_FIRST:
            send_1(d, False).start()

        s_in[y] = s_out[y]

    def queries():
        qkv_in[2].wait_recv()
        held["fq_t"] = feature(qx[...]).T

    def inside(h):
        keys_at = lax.broadcasted_iota(jnp.int32, (2 * TOK, 2 * TOK), 0)
        query_at = lax.broadcasted_iota(jnp.int32, (2 * TOK, 2 * TOK), 1)
        hs = slice(h * HD, (h + 1) * HD)
        scores = dot(held["fk"][:, hs], held["fq_t"][hs])
        weights = jnp.where(keys_at <= query_at, scores, 0.0).astype(BF16)
        mixed[hs] = dot(held["v_t"][hs], weights)

    def row_prefix():
        for d in FAR_FIRST:
            send_1(d, True).wait_recv()

        run = jnp.zeros((SL, HD), F32)
        for i in range(NY):
            e_buf[i] = run
            run = run + s_in[i].astype(F32)
        r_out[...] = run.astype(BF16)

        for d in FAR_FIRST:

            @pl.when(z + d < NZ)
            def _():
                send_2(d, False).start()

        r_in[z] = r_out[...]

    def all_prefix():
        for d in FAR_FIRST:

            @pl.when(z >= d)
            def _():
                send_2(d, True).wait_recv()

        before = jnp.zeros((SL, HD), F32)
        for i in range(NZ):
            before = before + jnp.where(i < z, r_in[i].astype(F32), 0.0)
        for i in range(NY):
            f_out[i] = (before + e_buf[i]).astype(BF16)

        for d in FAR_FIRST:
            send_3(d, False).start()

        pf[y] = f_out[y]

    def attend():
        fq_t = held['fq_t']
        gains = []
        for h in range(HEADS):
            at = pl.ds(pl.multiple_of(c * HALF + h * HD, HD), HD)
            turned = jnp.broadcast_to(gain[:, at], (HD, HD)).T
            gains.append(jnp.concatenate([turned, turned], axis=1))

        for d in FAR_FIRST:
            send_3(d, True).wait_recv()

        for h in range(HEADS):
            hs = slice(h * HD, (h + 1) * HD)
            at = pl.ds(pl.multiple_of(c * HALF + h * HD, HD), HD)
            prefix = pf[2 * h : 2 * h + 2].reshape(HD, HD)
            total = mixed[hs] + dot(prefix, fq_t[hs])
            scale = lax.rsqrt(jnp.mean(total * total, axis=0, keepdims=True) + 1e-05)
            attn[at] = (total * scale * gains[h]).astype(BF16)
            at_copy(h, c).start()

    def unit_a(i):
        zz = up(z, jnp.where(lax.rem(i, 2) == 1, lax.div(i + 1, 2), NZ - lax.div(i, 2)), NZ)
        return zz, lax.div(zz, 2), 0, lax.rem(zz, 2), lambda: wa[zz].reshape(NY * WB, 2 * HALF)

    def unit_b(rel, grp):
        xx = up(x, rel, NX)

        def blocks():
            found = []
            for zl in range(2):
                d = up(2 * xx + zl, NZ - z, NZ)
                slot = jnp.where(d <= 4, jnp.maximum(2 * d - 1, 0), 2 * NZ - 2 * d)
                for off in ORDER[4 * grp : 4 * grp + 4]:
                    found.append(wb[up(y, off % NY, NY), slot])
            return jnp.concatenate(found, axis=0)

        return NZ + 2 * xx + grp, xx, 1, grp, blocks

    def far_copy(n, i):
        rows = pl.ds(i * SL, SL)
        to = dev(z, y, c, x_dn if i else x_up)
        return remote(near.at[n, :, rows], got.at[n, i], s_far.at[n, i], r_far.at[n, i], to)

    def near_copy(n, kind, idx, way, core):
        to = dev(z, y, core, jnp.where(way == 0, x_up, x_dn))
        return remote(
            near.at[n, core], fin.at[c, kind, idx, way], s_near.at[n, core],
            r_fin.at[((c * 2 + kind) * 2 + idx) * 2 + way], to,
        )

    def sib_copy(n, kind, idx):
        i = kind * 2 + idx
        return remote(near.at[n, 1 - c], sib.at[i], s_near.at[n, 0], r_sib.at[i], sibling)

    def far_unit(n, xx, kind, idx, blocks):
        @pl.when(up(xx, NX - x, NX) == 2)
        def _():
            total = dot(blocks(), attn[...]).astype(BF16)
            for core in range(2):
                near[n, core] = total[:, core * TOK : (core + 1) * TOK]
            for i in range(2):
                far_copy(n, i).start()

    def near_unit(n, xx, kind, idx, blocks):
        rel = up(xx, NX - x, NX)

        @pl.when(lax.rem(rel, 2) == 1)
        def _():
            total = dot(blocks(), attn[...])
            way = lax.div(rel, 2)
            rows = pl.ds(pl.multiple_of(way * SL, SL), SL)
            for core in range(2):
                part[core] = total[:, core * TOK : (core + 1) * TOK]
                near[n, core] = part[core].astype(BF16)
            far_copy_in = remote(got.at[n, way], got.at[n, way], s_far.at[n, way], r_far.at[n, way], sibling)
            far_copy_in.wait_recv()
            for core in range(2):
                near[n, core, rows] = (part[core, rows] + got[n, way, core].astype(F32)).astype(BF16)
                near_copy(n, kind, idx, way, core).start()

        @pl.when(rel == 0)
        def _():
            total = dot(blocks(), attn[...]).astype(BF16)
            for core in range(2):
                near[n, core] = total[:, core * TOK : (core + 1) * TOK]
            sib_copy(n, kind, idx).start()

    def far_units(first, last, grp):
        @pl.loop(first, last)
        def _(i):
            far_unit(*unit_a(i))

        far_unit(*unit_b(2, grp))

    def near_units(first, last, grp):
        @pl.loop(first, last)
        def _(i):
            near_unit(*unit_a(i))

        for rel in (1, 3, 0):
            near_unit(*unit_b(rel, grp))

    def line_1():
        line_recv(1)
        ring_send(1, 1)

    def line_2():
        line_recv(2)
        line_send(3)
        line_send(4)
        ring_send(1, 2)

    def line_3():
        line_recv(3)
        ring_send(1, 3)
        line_recv(4)
        ring_send(1, 4)

    def swap():
        for h in range(HEADS):
            at_copy(h, 1 - c).wait_recv()

    def early_far():
        far_units(0, 5, 0)

    def early_near():
        near_units(0, 5, 0)

    def late_far():
        far_units(5, NZ, 1)

    def late_near():
        near_units(5, NZ, 1)

    def rings(*pairs):
        for pair in pairs:
            ring_recv(*pair)

    states()
    line_1()
    queries()
    line_2()
    rings((1, 1),)
    inside(0)
    line_3()
    rings((1, 2),)
    inside(1)
    row_prefix()
    rings((1, 3),)
    inside(2)
    rings((1, 4),)
    inside(3)
    rings((1, 0),)
    rings((2, 1),)
    all_prefix()
    rings((2, 2),)
    rings((2, 3),)
    rings((2, 4),)
    rings((3, 1),)
    rings((2, 0),)
    attend()
    rings((3, 2),)
    rings((3, 3),)
    rings((3, 4),)
    rings((3, 0),)
    swap()
    early_far()
    rings((4, 1),)
    rings((4, 2),)
    rings((4, 0),)
    rings((4, 3),)
    rings((4, 4),)
    late_far()
    early_near()
    late_near()
    for kind, idx in ((1, 0), (0, 0), (0, 1), (1, 1)):
        n = 2 * x + idx + kind * NZ
        away = sib.at[kind * 2 + idx]
        remote(away, away, s_near.at[0, 0], r_sib.at[kind * 2 + idx], sibling).wait_recv()
        for s in range(2):
            for way in range(2):
                ref = fin.at[s, kind, idx, way]
                i = ((s * 2 + kind) * 2 + idx) * 2 + way
                remote(ref, ref, s_near.at[0, 0], r_fin.at[i], sibling).wait_recv()
            own = jnp.where(s == c, near[n, c].astype(F32), sib[kind * 2 + idx].astype(F32))
            total = own + fin[s, kind, idx, 0].astype(F32) + fin[s, kind, idx, 1].astype(F32)
            for i in range(NY):
                zl, off = (idx, ORDER[i]) if kind == 0 else (i // 4, ORDER[4 * idx + i % 4])
                out_t[zl * NY + up(y, off % NY, NY), 2 * s + kind] = total[i * WB : (i + 1) * WB]
    for j in range(NY):
        o_ref[:, j * HD : (j + 1) * HD] = out_t[2 * j : 2 * j + 2].reshape(HD, HD).T.astype(BF16)

    for copy in qkv:
        copy.wait_send()

    @pl.loop(1, NY)
    def _(d):
        send_1(d, False).wait_send()
        send_3(d, False).wait_send()

        @pl.when(z + d < NZ)
        def _():
            send_2(d, False).wait_send()

    for kind, way in both:
        for k in range(1, 5):
            if k < 4 or kind == way:
                line(kind, way, k, False).wait_send()
        for step in range(1, 5):
            for group in range(5):
                if step < 4 or group in LAST[kind][way]:
                    ring(kind, way, step, group, False).wait_send()
    for h in range(HEADS):
        at_copy(h, c).wait_send()

    def unit_left(n, xx, kind, idx, blocks):
        rel = up(xx, NX - x, NX)

        @pl.when(rel == 2)
        def _():
            for i in range(2):
                far_copy(n, i).wait_send()

        @pl.when(lax.rem(rel, 2) == 1)
        def _():
            for core in range(2):
                near_copy(n, kind, idx, lax.div(rel, 2), core).wait_send()

        @pl.when(rel == 0)
        def _():
            sib_copy(n, kind, idx).wait_send()

    @pl.loop(0, NZ)
    def _(i):
        unit_left(*unit_a(i))

    for rel in range(NX):
        for grp in range(2):
            unit_left(*unit_b(rel, grp))


def per_device(queries, keys, values, head_gain, w_out):
    dma = pltpu.SemaphoreType.DMA
    vmem = pltpu.VMEM
    rows = NY * WB
    scratch = [
        vmem((1, 2 * HALF), F32),
        vmem((NZ, NY, WB, 2 * HALF), BF16),
        vmem((NY, NZ, WB, 2 * HALF), BF16),
        vmem((2 * TOK, HALF), BF16),
        vmem((2 * TOK, HALF), BF16),
        vmem((2 * TOK, HALF), BF16),
        vmem((NY, SL, HD), BF16),
        vmem((NY, SL, HD), BF16),
        vmem((NY, SL, HD), F32),
        vmem((SL, HD), BF16),
        vmem((NZ, SL, HD), BF16),
        vmem((NY, SL, HD), BF16),
        vmem((NY, SL, HD), BF16),
        vmem((HALF, 2 * TOK), F32),
        vmem((2 * HALF, 2 * TOK), BF16),
        vmem((16, 2, rows, TOK), BF16),
        vmem((16, 2, 2, SL, TOK), BF16),
        vmem((2, 2, 2, 2, rows, TOK), BF16),
        vmem((4, rows, TOK), BF16),
        vmem((2, rows, TOK), F32),
        vmem((2 * NY, 4, WB, TOK), F32),
        dma((6,)),
        dma((3,)), dma((3,)),
        dma((16,)), dma((16,)), dma((80,)), dma((80,)),
        dma((8,)), dma((8,)), dma((8,)), dma((8,)), dma((8,)), dma((8,)),
        dma((HEADS,)), dma((HEADS,)),
        dma((16, 2)), dma((16, 2)), dma((16, 2)),
        dma((16,)), dma((4,)),
    ]
    operands = (queries, keys, values, head_gain.reshape(1, -1), w_out.T)
    return pl.pallas_call(
        kernel,
        out_shape=jax.ShapeDtypeStruct(queries.shape, BF16),
        in_specs=[pl.BlockSpec(memory_space=pl.ANY)] * 5,
        out_specs=pl.BlockSpec(memory_space=pltpu.VMEM),
        scratch_shapes=scratch,
        compiler_params=pltpu.CompilerParams(
            collective_id=0, has_side_effects=True, vmem_limit_bytes=48 * 2**20
        ),
        cost_estimate=pl.CostEstimate(flops=2**31, bytes_accessed=2**21, transcendentals=2**19),
    )(*[pltpu.with_memory_space_constraint(a, pltpu.HBM) for a in operands])


def solution(mesh):
    placed = (P("ctx", "head"), P("ctx", "head"), P("ctx", "head"), P("head"), P("head", "ctx"))
    return jax.shard_map(
        per_device, mesh=mesh, in_specs=placed, out_specs=P("ctx", "head"), check_vma=False
    )
```

```python
import jax
import jax.numpy as jnp
from jax import lax
from jax.experimental import pallas as pl
from jax.experimental.pallas import tpu as pltpu
from jax.sharding import PartitionSpec as P

NZ, NY, NX = 8, 8, 4
HD = 128
TOK = 128
HALF = 512
HEADS = HALF // HD
SL = 64
WB = 16
GROUPS = ((0, 1), (1, 2), (3, 2), (5, 2), (7, 1))
LAST = (((0, 1, 2), (3, 4)), ((3, 4), (0, 1, 2)))
ORDER = (0, 1, -1, 2, -2, 3, -3, 4)
FAR_FIRST = (4, 3, 5, 2, 6, 1, 7)
F32, BF16 = jnp.float32, jnp.bfloat16


def slot_of(rel):
    return 2 * rel - 1 if rel > 0 else -2 * rel


def feature(x):
    x = x.astype(F32)
    return jnp.where(x > 0.0, x + 1.0, jnp.exp(jnp.minimum(x, 0.0))).astype(BF16)


def dot(a, b):
    return jnp.dot(a, b, preferred_element_type=F32)


def up(a, d, n):
    return lax.rem(a + d, n)


def down(a, d, n):
    return lax.rem(a + n - d, n)


def kernel(
    q_ref, k_ref, v_ref, g_ref, w_ref, o_ref,
    gain, wa, wb, qx, kx, vx, fq_t, fk_s, v_t, s_out, s_in, e_buf, r_out, r_in, f_out, pf, mixed, attn,
    near, got, fin, sib, part, keep, out_t,
    s_in0, s_qkv, r_qkv, s_line, r_line, s_ring, r_ring,
    s_p1, r_p1, s_p2, r_p2, s_p3, r_p3, s_at, r_at, s_far, r_far, s_near, r_fin, r_sib,
):
    me = lax.axis_index("ctx")
    x = lax.axis_index("head")
    c = lax.rem(me, 2)
    p = lax.div(me, 2)
    y = lax.rem(p, NY)
    z = lax.div(p, NY)

    def dev(zz, yy, cc, xx):
        return ((zz * NY + yy) * 2 + cc, xx)

    def remote(src, dst, ss, rs, to):
        return pltpu.make_async_remote_copy(
            src_ref=src, dst_ref=dst, send_sem=ss, recv_sem=rs,
            device_id=to, device_id_type=pl.DeviceIdType.MESH,
        )

    sibling = dev(z, y, 1 - c, x)
    x_up, x_dn = up(x, 1, NX), down(x, 1, NX)

    mine = pl.ds(pl.multiple_of(c * TOK, TOK), TOK)
    other = pl.ds(pl.multiple_of((1 - c) * TOK, TOK), TOK)
    cols = pl.ds(pl.multiple_of(c * HALF, HALF), HALF)
    cols_other = pl.ds(pl.multiple_of((1 - c) * HALF, HALF), HALF)
    qkv_refs = ((k_ref, kx), (v_ref, vx), (q_ref, qx))
    inputs = [
        pltpu.make_async_copy(w_ref.at[pl.ds(0, WB)], wa.at[z, 0], s_in0.at[0]),
        pltpu.make_async_copy(w_ref.at[pl.ds(WB, WB)], wb.at[y, 0], s_in0.at[1]),
    ]
    for i, (src, dst) in enumerate(qkv_refs):
        inputs.append(pltpu.make_async_copy(src.at[:, cols], dst.at[mine], s_in0.at[2 + i]))
    inputs.append(pltpu.make_async_copy(g_ref, gain, s_in0.at[5]))
    for copy in inputs:
        copy.start()

    barrier = pltpu.get_barrier_semaphore()

    def greet(to):
        pl.semaphore_signal(barrier, inc=1, device_id=to, device_id_type=pl.DeviceIdType.MESH)

    greet(sibling)

    @pl.loop(1, NY)
    def _(d):
        greet(dev(z, up(y, d, NY), c, x))

    @pl.loop(1, NZ)
    def _(d):
        greet(dev(up(z, d, NZ), y, c, x))

    for xx in (x_up, x_dn):
        for cc in range(2):
            greet(dev(z, y, cc, xx))

    def at_y(yy):
        return dev(z, yy, c, x)

    def at_z(zz):
        return dev(zz, y, c, x)

    kinds = ((wa, y, z, at_y, at_z), (wb, z, y, at_z, at_y))

    def line(kind, way, k, arriving):
        buf, u, t, at_u, _ = kinds[kind]
        sign = 1 if way else -1
        rel = 4 if k == 4 else sign * k
        dst = buf.at[t, slot_of(rel)]
        hop = (1, 2, 1, 2)[k - 1]
        src = dst if arriving else buf.at[t, slot_of(sign * (k - hop))]
        if not arriving and k < 3:
            src = w_ref.at[pl.ds(kind * WB, WB)]
        i = (kind * 2 + way) * 4 + k - 1
        to = at_u(down(u, hop, NY) if way else up(u, hop, NY))
        return remote(src, dst, s_line.at[i], r_line.at[i], to)

    def ring(kind, way, step, group, arriving):
        buf, _, t, _, at_t = kinds[kind]
        gap = step if arriving else step - 1
        row = up(t, gap, NZ) if way else down(t, gap, NZ)
        ref = buf.at[row, pl.ds(*GROUPS[group])]
        src = ref
        if step == 1 and group == 0 and not arriving:
            ref = buf.at[row, 0]
            src = w_ref.at[pl.ds(kind * WB, WB)]
        i = ((kind * 2 + way) * 4 + step - 1) * 5 + group
        to = at_t(down(t, 1, NZ) if way else up(t, 1, NZ))
        return remote(src, ref, s_ring.at[i], r_ring.at[i], to)

    both = [(kind, way) for kind in range(2) for way in range(2)]

    def ring_send(step, group):
        for kind, way in both:
            if step < 4 or group in LAST[kind][way]:
                ring(kind, way, step, group, False).start()

    def ring_recv(step, group, kinds_now=(0, 1)):
        for kind, way in [pair for pair in both if pair[0] in kinds_now]:
            if step < 4 or group in LAST[kind][way]:
                ring(kind, way, step, group, True).wait_recv()
                if step < 3 or (step == 3 and group in LAST[kind][way]):
                    ring(kind, way, step + 1, group, False).start()

    def line_send(k):
        for kind, way in both:
            if k < 4 or kind == way:
                line(kind, way, k, False).start()

    def line_recv(k):
        for kind, way in both:
            if k < 4 or kind == way:
                line(kind, way, k, True).wait_recv()

    pl.semaphore_wait(barrier, 1 + (NY - 1) + (NZ - 1) + 4)

    qkv = [
        remote(src.at[:, cols_other], dst.at[mine], s_qkv.at[i], r_qkv.at[i], sibling)
        for i, (src, dst) in enumerate(qkv_refs)
    ]
    qkv_in = [
        remote(src.at[:, cols_other], dst.at[other], s_qkv.at[i], r_qkv.at[i], sibling)
        for i, (src, dst) in enumerate(qkv_refs)
    ]
    for copy in qkv:
        copy.start()
    ring_send(1, 0)
    line_send(1)
    line_send(2)

    def send_1(d, arriving):
        yy = down(y, d, NY) if arriving else up(y, d, NY)
        slot = s_in.at[yy if arriving else y]
        return remote(s_out.at[yy], slot, s_p1.at[d], r_p1.at[d], dev(z, yy, c, x))

    def send_2(d, arriving):
        zz = down(z, d, NZ) if arriving else up(z, d, NZ)
        slot = r_in.at[zz if arriving else z]
        return remote(r_out, slot, s_p2.at[d], r_p2.at[d], dev(zz, y, c, x))

    def send_3(d, arriving):
        yy = down(y, d, NY) if arriving else up(y, d, NY)
        slot = pf.at[yy if arriving else y]
        return remote(f_out.at[yy], slot, s_p3.at[d], r_p3.at[d], dev(z, yy, c, x))

    def at_copy(h, who):
        ref = attn.at[pl.ds(pl.multiple_of(who * HALF + h * HD, HD), HD)]
        return remote(ref, ref, s_at.at[h], r_at.at[h], sibling)

    def turn(tokens):
        fk_s[tokens] = feature(kx[tokens])
        v_t[:, tokens] = vx[tokens].T

    def states():
        for copy in inputs:
            copy.wait()
        turn(mine)
        fq_t[:, mine] = feature(qx[mine]).T
        qkv_in[0].wait_recv()
        qkv_in[1].wait_recv()
        turn(other)
        for h in range(HEADS):
            hs = slice(h * HD, (h + 1) * HD)
            state = dot(v_t[hs], fk_s[:, hs]).astype(BF16)
            s_out[2 * h] = state[:SL]
            s_out[2 * h + 1] = state[SL:]

        for d in FAR_FIRST:
            send_1(d, False).start()

        s_in[y] = s_out[y]

    def queries():
        qkv_in[2].wait_recv()
        fq_t[:, other] = feature(qx[other]).T

    def inside(h):
        keys_at = lax.broadcasted_iota(jnp.int32, (2 * TOK, 2 * TOK), 0)
        query_at = lax.broadcasted_iota(jnp.int32, (2 * TOK, 2 * TOK), 1)
        hs = slice(h * HD, (h + 1) * HD)
        scores = dot(fk_s[:, hs], fq_t[hs])
        weights = jnp.where(keys_at <= query_at, scores, 0.0).astype(BF16)
        mixed[hs] = dot(v_t[hs], weights)

    def row_prefix():
        for d in FAR_FIRST:
            send_1(d, True).wait_recv()

        run = jnp.zeros((SL, HD), F32)
        for i in range(NY):
            e_buf[i] = run
            run = run + s_in[i].astype(F32)
        r_out[...] = run.astype(BF16)

        for d in FAR_FIRST:

            @pl.when(z + d < NZ)
            def _():
                send_2(d, False).start()

        r_in[z] = r_out[...]

    def all_prefix():
        for d in FAR_FIRST:

            @pl.when(z >= d)
            def _():
                send_2(d, True).wait_recv()

        before = jnp.zeros((SL, HD), F32)
        for i in range(NZ):
            before = before + jnp.where(i < z, r_in[i].astype(F32), 0.0)
        for i in range(NY):
            f_out[i] = (before + e_buf[i]).astype(BF16)

        for d in FAR_FIRST:
            send_3(d, False).start()

        pf[y] = f_out[y]

    def attend():
        gains = []
        for h in range(HEADS):
            at = pl.ds(pl.multiple_of(c * HALF + h * HD, HD), HD)
            turned = jnp.broadcast_to(gain[:, at], (HD, HD)).T
            gains.append(jnp.concatenate([turned, turned], axis=1))

        for d in FAR_FIRST:
            send_3(d, True).wait_recv()

        for h in range(HEADS):
            hs = slice(h * HD, (h + 1) * HD)
            at = pl.ds(pl.multiple_of(c * HALF + h * HD, HD), HD)
            prefix = pf[2 * h : 2 * h + 2].reshape(HD, HD)
            total = mixed[hs] + dot(prefix, fq_t[hs])
            scale = lax.rsqrt(jnp.mean(total * total, axis=0, keepdims=True) + 1e-05)
            attn[at] = (total * scale * gains[h]).astype(BF16)
            at_copy(h, c).start()

    def unit_a(i):
        zz = up(z, jnp.where(lax.rem(i, 2) == 1, lax.div(i + 1, 2), NZ - lax.div(i, 2)), NZ)
        return zz, lax.div(zz, 2), 0, lax.rem(zz, 2), lambda: wa[zz].reshape(NY * WB, 2 * HALF)

    def unit_b(rel, grp):
        xx = up(x, rel, NX)

        def blocks():
            found = []
            for zl in range(2):
                d = up(2 * xx + zl, NZ - z, NZ)
                slot = jnp.where(d <= 4, jnp.maximum(2 * d - 1, 0), 2 * NZ - 2 * d)
                for off in ORDER[4 * grp : 4 * grp + 4]:
                    found.append(wb[up(y, off % NY, NY), slot])
            return jnp.concatenate(found, axis=0)

        return NZ + 2 * xx + grp, xx, 1, grp, blocks

    def far_copy(n, i):
        rows = pl.ds(i * SL, SL)
        to = dev(z, y, c, x_dn if i else x_up)
        return remote(near.at[n, :, rows], got.at[n, i], s_far.at[n, i], r_far.at[n, i], to)

    def rows_of(half):
        return pl.ds(pl.multiple_of(half * SL, SL), SL)

    def near_copy(n, kind, idx, way, core, half):
        to = dev(z, y, core, jnp.where(way == 0, x_up, x_dn))
        rows = rows_of(half)
        return remote(
            near.at[n, core, rows], fin.at[c, kind, idx, way, rows], s_near.at[n, core, half],
            r_fin.at[((c * 2 + kind) * 2 + idx) * 2 + way, half], to,
        )

    def sib_copy(n, kind, idx):
        i = kind * 2 + idx
        return remote(near.at[n, 1 - c], sib.at[i], s_near.at[n, 0, 0], r_sib.at[i], sibling)

    def far_unit(n, xx, kind, idx, blocks):
        @pl.when(up(xx, NX - x, NX) == 2)
        def _():
            total = dot(blocks(), attn[...]).astype(BF16)
            for core in range(2):
                near[n, core] = total[:, core * TOK : (core + 1) * TOK]
            for i in range(2):
                far_copy(n, i).start()

    def near_unit(n, xx, kind, idx, blocks):
        rel = up(xx, NX - x, NX)

        @pl.when(lax.rem(rel, 2) == 1)
        def _():
            total = dot(blocks(), attn[...])
            way = lax.div(rel, 2)
            for core in range(2):
                part[core] = total[:, core * TOK : (core + 1) * TOK]
                near[n, core] = part[core].astype(BF16)
                keep[n, core] = part[core, rows_of(way)]
                near_copy(n, kind, idx, way, core, 1 - way).start()

        @pl.when(rel == 0)
        def _():
            total = dot(blocks(), attn[...]).astype(BF16)
            for core in range(2):
                near[n, core] = total[:, core * TOK : (core + 1) * TOK]
            sib_copy(n, kind, idx).start()

    def sum_unit(n, xx, kind, idx, blocks):
        rel = up(xx, NX - x, NX)

        @pl.when(lax.rem(rel, 2) == 1)
        def _():
            way = lax.div(rel, 2)
            ref = got.at[n, way]
            remote(ref, ref, s_far.at[n, way], r_far.at[n, way], sibling).wait_recv()
            for core in range(2):
                near[n, core, rows_of(way)] = (keep[n, core] + got[n, way, core].astype(F32)).astype(BF16)
                near_copy(n, kind, idx, way, core, way).start()

    def far_units(first, last, grp):
        @pl.loop(first, last)
        def _(i):
            far_unit(*unit_a(i))

        far_unit(*unit_b(2, grp))

    def near_units(first, last, grp):
        @pl.loop(first, last)
        def _(i):
            near_unit(*unit_a(i))

        for rel in (1, 3, 0):
            near_unit(*unit_b(rel, grp))

    def sum_units(first, last, grp):
        @pl.loop(first, last)
        def _(i):
            sum_unit(*unit_a(i))

        for rel in (1, 3):
            sum_unit(*unit_b(rel, grp))

    def line_1():
        line_recv(1)
        ring_send(1, 1)

    def line_2():
        line_recv(2)
        line_send(3)
        line_send(4)
        ring_send(1, 2)

    def line_3():
        line_recv(3)
        ring_send(1, 3)
        line_recv(4)
        ring_send(1, 4)

    def swap():
        for h in range(HEADS):
            at_copy(h, 1 - c).wait_recv()

    def early_far():
        far_units(0, 5, 0)

    def early_near():
        near_units(0, 5, 0)

    def late_far():
        far_units(5, NZ, 1)

    def late_near():
        near_units(5, NZ, 1)

    def early_sum():
        sum_units(0, 5, 0)

    def late_sum():
        sum_units(5, NZ, 1)

    def rings(*pairs):
        for pair in pairs:
            ring_recv(*pair)

    states()
    line_1()
    queries()
    line_2()
    ring_recv(1, 1)
    inside(0)
    line_3()
    ring_recv(1, 2)
    inside(1)
    row_prefix()
    ring_recv(1, 3)
    inside(2)
    ring_recv(1, 4)
    inside(3)
    ring_recv(1, 0)
    ring_recv(2, 1)
    all_prefix()
    ring_recv(2, 2)
    ring_recv(2, 3)
    ring_recv(2, 4)
    ring_recv(3, 1)
    ring_recv(2, 0)
    attend()
    ring_recv(3, 2)
    ring_recv(3, 3)
    ring_recv(3, 4)
    ring_recv(3, 0)
    swap()
    early_far()
    ring_recv(4, 1)
    ring_recv(4, 2)
    ring_recv(4, 0)
    ring_recv(4, 3)
    ring_recv(4, 4)
    late_far()
    early_near()
    late_near()
    early_sum()
    late_sum()
    for kind, idx in ((1, 0), (0, 0), (0, 1), (1, 1)):
        n = 2 * x + idx + kind * NZ
        away = sib.at[kind * 2 + idx]
        remote(away, away, s_near.at[0, 0, 0], r_sib.at[kind * 2 + idx], sibling).wait_recv()
        for s in range(2):
            for way in range(2):
                i = ((s * 2 + kind) * 2 + idx) * 2 + way
                for half in range(2):
                    ref = fin.at[s, kind, idx, way, pl.ds(half * SL, SL)]
                    remote(ref, ref, s_near.at[0, 0, 0], r_fin.at[i, half], sibling).wait_recv()
            own = jnp.where(s == c, near[n, c].astype(F32), sib[kind * 2 + idx].astype(F32))
            total = own + fin[s, kind, idx, 0].astype(F32) + fin[s, kind, idx, 1].astype(F32)
            for i in range(NY):
                zl, off = (idx, ORDER[i]) if kind == 0 else (i // 4, ORDER[4 * idx + i % 4])
                out_t[zl * NY + up(y, off % NY, NY), 2 * s + kind] = total[i * WB : (i + 1) * WB]
    for j in range(NY):
        o_ref[:, j * HD : (j + 1) * HD] = out_t[2 * j : 2 * j + 2].reshape(HD, HD).T.astype(BF16)

    for copy in qkv:
        copy.wait_send()

    @pl.loop(1, NY)
    def _(d):
        send_1(d, False).wait_send()
        send_3(d, False).wait_send()

        @pl.when(z + d < NZ)
        def _():
            send_2(d, False).wait_send()

    for kind, way in both:
        for k in range(1, 5):
            if k < 4 or kind == way:
                line(kind, way, k, False).wait_send()
        for step in range(1, 5):
            for group in range(5):
                if step < 4 or group in LAST[kind][way]:
                    ring(kind, way, step, group, False).wait_send()
    for h in range(HEADS):
        at_copy(h, c).wait_send()

    def unit_left(n, xx, kind, idx, blocks):
        rel = up(xx, NX - x, NX)

        @pl.when(rel == 2)
        def _():
            for i in range(2):
                far_copy(n, i).wait_send()

        @pl.when(lax.rem(rel, 2) == 1)
        def _():
            for core in range(2):
                for half in range(2):
                    near_copy(n, kind, idx, lax.div(rel, 2), core, half).wait_send()

        @pl.when(rel == 0)
        def _():
            sib_copy(n, kind, idx).wait_send()

    @pl.loop(0, NZ)
    def _(i):
        unit_left(*unit_a(i))

    for rel in range(NX):
        for grp in range(2):
            unit_left(*unit_b(rel, grp))


def per_device(queries, keys, values, head_gain, w_out):
    dma = pltpu.SemaphoreType.DMA
    vmem = pltpu.VMEM
    rows = NY * WB
    scratch = [
        vmem((1, 2 * HALF), F32),
        vmem((NZ, NY, WB, 2 * HALF), BF16),
        vmem((NY, NZ, WB, 2 * HALF), BF16),
        vmem((2 * TOK, HALF), BF16),
        vmem((2 * TOK, HALF), BF16),
        vmem((2 * TOK, HALF), BF16),
        vmem((HALF, 2 * TOK), BF16),
        vmem((2 * TOK, HALF), BF16),
        vmem((HALF, 2 * TOK), BF16),
        vmem((NY, SL, HD), BF16),
        vmem((NY, SL, HD), BF16),
        vmem((NY, SL, HD), F32),
        vmem((SL, HD), BF16),
        vmem((NZ, SL, HD), BF16),
        vmem((NY, SL, HD), BF16),
        vmem((NY, SL, HD), BF16),
        vmem((HALF, 2 * TOK), F32),
        vmem((2 * HALF, 2 * TOK), BF16),
        vmem((16, 2, rows, TOK), BF16),
        vmem((16, 2, 2, SL, TOK), BF16),
        vmem((2, 2, 2, 2, rows, TOK), BF16),
        vmem((4, rows, TOK), BF16),
        vmem((2, rows, TOK), F32),
        vmem((16, 2, SL, TOK), F32),
        vmem((2 * NY, 4, WB, TOK), F32),
        dma((6,)),
        dma((3,)), dma((3,)),
        dma((16,)), dma((16,)), dma((80,)), dma((80,)),
        dma((8,)), dma((8,)), dma((8,)), dma((8,)), dma((8,)), dma((8,)),
        dma((HEADS,)), dma((HEADS,)),
        dma((16, 2)), dma((16, 2)), dma((16, 2, 2)),
        dma((16, 2)), dma((4,)),
    ]
    operands = (queries, keys, values, head_gain.reshape(1, -1), w_out.T)
    return pl.pallas_call(
        kernel,
        out_shape=jax.ShapeDtypeStruct(queries.shape, BF16),
        in_specs=[pl.BlockSpec(memory_space=pl.ANY)] * 5,
        out_specs=pl.BlockSpec(memory_space=pltpu.VMEM),
        scratch_shapes=scratch,
        compiler_params=pltpu.CompilerParams(
            collective_id=0, has_side_effects=True, vmem_limit_bytes=48 * 2**20
        ),
        cost_estimate=pl.CostEstimate(flops=2**31, bytes_accessed=2**21, transcendentals=2**19),
    )(*[pltpu.with_memory_space_constraint(a, pltpu.HBM) for a in operands])


def solution(mesh):
    placed = (P("ctx", "head"), P("ctx", "head"), P("ctx", "head"), P("head"), P("head", "ctx"))
    return jax.shard_map(
        per_device, mesh=mesh, in_specs=placed, out_specs=P("ctx", "head"), check_vma=False
    )
```

```python
import jax
import jax.numpy as jnp
from jax import lax
from jax.experimental import pallas as pl
from jax.experimental.pallas import tpu as pltpu
from jax.sharding import PartitionSpec as P

NZ, NY, NX = 8, 8, 4
HD = 128
TOK = 128
HALF = 512
HEADS = HALF // HD
SL = 64
WB = 16
GROUPS = ((0, 1), (1, 2), (3, 2), (5, 2), (7, 1))
LAST = (((0, 1, 2), (3, 4)), ((3, 4), (0, 1, 2)))
ORDER = (0, 1, -1, 2, -2, 3, -3, 4)
FAR_FIRST = (4, 3, 5, 2, 6, 1, 7)
F32, BF16 = jnp.float32, jnp.bfloat16


def slot_of(rel):
    return 2 * rel - 1 if rel > 0 else -2 * rel


def feature(x):
    x = x.astype(F32)
    return jnp.where(x > 0.0, x + 1.0, jnp.exp(jnp.minimum(x, 0.0))).astype(BF16)


def dot(a, b):
    return jnp.dot(a, b, preferred_element_type=F32)


def up(a, d, n):
    return lax.rem(a + d, n)


def down(a, d, n):
    return lax.rem(a + n - d, n)


def kernel(
    q_ref, k_ref, v_ref, g_ref, w_ref, o_ref,
    gain, wa, wb, qx, kx, vx, fq_t, fk_s, v_t, s_out, s_in, e_buf, r_out, r_in, f_out, pf, mixed, attn,
    near, got, fin, sib, part, keep, out_t,
    s_in0, s_qkv, r_qkv, s_line, r_line, s_ring, r_ring,
    s_p1, r_p1, s_p2, r_p2, s_p3, r_p3, s_at, r_at, s_far, r_far, s_near, r_fin, r_sib,
):
    me = lax.axis_index("ctx")
    x = lax.axis_index("head")
    c = lax.rem(me, 2)
    p = lax.div(me, 2)
    y = lax.rem(p, NY)
    z = lax.div(p, NY)

    def dev(zz, yy, cc, xx):
        return ((zz * NY + yy) * 2 + cc, xx)

    def remote(src, dst, ss, rs, to):
        return pltpu.make_async_remote_copy(
            src_ref=src, dst_ref=dst, send_sem=ss, recv_sem=rs,
            device_id=to, device_id_type=pl.DeviceIdType.MESH,
        )

    sibling = dev(z, y, 1 - c, x)
    x_up, x_dn = up(x, 1, NX), down(x, 1, NX)

    mine = pl.ds(pl.multiple_of(c * TOK, TOK), TOK)
    other = pl.ds(pl.multiple_of((1 - c) * TOK, TOK), TOK)
    cols = pl.ds(pl.multiple_of(c * HALF, HALF), HALF)
    cols_other = pl.ds(pl.multiple_of((1 - c) * HALF, HALF), HALF)
    qkv_refs = ((k_ref, kx), (v_ref, vx), (q_ref, qx))
    inputs = [
        pltpu.make_async_copy(w_ref.at[pl.ds(0, WB)], wa.at[z, 0], s_in0.at[0]),
        pltpu.make_async_copy(w_ref.at[pl.ds(WB, WB)], wb.at[y, 0], s_in0.at[1]),
    ]
    for i, (src, dst) in enumerate(qkv_refs):
        inputs.append(pltpu.make_async_copy(src.at[:, cols], dst.at[mine], s_in0.at[2 + i]))
    inputs.append(pltpu.make_async_copy(g_ref, gain, s_in0.at[5]))
    for copy in inputs:
        copy.start()

    barrier = pltpu.get_barrier_semaphore()

    def greet(to):
        pl.semaphore_signal(barrier, inc=1, device_id=to, device_id_type=pl.DeviceIdType.MESH)

    greet(sibling)

    @pl.loop(1, NY)
    def _(d):
        greet(dev(z, up(y, d, NY), c, x))

    @pl.loop(1, NZ)
    def _(d):
        greet(dev(up(z, d, NZ), y, c, x))

    for xx in (x_up, x_dn):
        for cc in range(2):
            greet(dev(z, y, cc, xx))

    def at_y(yy):
        return dev(z, yy, c, x)

    def at_z(zz):
        return dev(zz, y, c, x)

    kinds = ((wa, y, z, at_y, at_z), (wb, z, y, at_z, at_y))

    def line(kind, way, k, arriving):
        buf, u, t, at_u, _ = kinds[kind]
        sign = 1 if way else -1
        rel = 4 if k == 4 else sign * k
        dst = buf.at[t, slot_of(rel)]
        hop = (1, 2, 1, 2)[k - 1]
        src = dst if arriving else buf.at[t, slot_of(sign * (k - hop))]
        if not arriving and k < 3:
            src = w_ref.at[pl.ds(kind * WB, WB)]
        i = (kind * 2 + way) * 4 + k - 1
        to = at_u(down(u, hop, NY) if way else up(u, hop, NY))
        return remote(src, dst, s_line.at[i], r_line.at[i], to)

    def ring(kind, way, step, group, arriving):
        buf, _, t, _, at_t = kinds[kind]
        gap = step if arriving else step - 1
        row = up(t, gap, NZ) if way else down(t, gap, NZ)
        ref = buf.at[row, pl.ds(*GROUPS[group])]
        src = ref
        if step == 1 and group == 0 and not arriving:
            ref = buf.at[row, 0]
            src = w_ref.at[pl.ds(kind * WB, WB)]
        i = ((kind * 2 + way) * 4 + step - 1) * 5 + group
        to = at_t(down(t, 1, NZ) if way else up(t, 1, NZ))
        return remote(src, ref, s_ring.at[i], r_ring.at[i], to)

    both = [(kind, way) for kind in range(2) for way in range(2)]

    def ring_send(step, group):
        for kind, way in both:
            if step < 4 or group in LAST[kind][way]:
                ring(kind, way, step, group, False).start()

    def ring_recv(step, group, kinds_now=(0, 1)):
        for kind, way in [pair for pair in both if pair[0] in kinds_now]:
            if step < 4 or group in LAST[kind][way]:
                ring(kind, way, step, group, True).wait_recv()
                if step < 3 or (step == 3 and group in LAST[kind][way]):
                    ring(kind, way, step + 1, group, False).start()

    def line_send(k):
        for kind, way in both:
            if k < 4 or kind == way:
                line(kind, way, k, False).start()

    def line_recv(k):
        for kind, way in both:
            if k < 4 or kind == way:
                line(kind, way, k, True).wait_recv()

    pl.semaphore_wait(barrier, 1 + (NY - 1) + (NZ - 1) + 4)

    qkv = [
        remote(src.at[:, cols_other], dst.at[mine], s_qkv.at[i], r_qkv.at[i], sibling)
        for i, (src, dst) in enumerate(qkv_refs)
    ]
    qkv_in = [
        remote(src.at[:, cols_other], dst.at[other], s_qkv.at[i], r_qkv.at[i], sibling)
        for i, (src, dst) in enumerate(qkv_refs)
    ]
    for copy in qkv:
        copy.start()
    ring_send(1, 0)
    line_send(1)
    line_send(2)

    def send_1(d, arriving):
        yy = down(y, d, NY) if arriving else up(y, d, NY)
        slot = s_in.at[yy if arriving else y]
        return remote(s_out.at[yy], slot, s_p1.at[d], r_p1.at[d], dev(z, yy, c, x))

    def send_2(d, arriving):
        zz = down(z, d, NZ) if arriving else up(z, d, NZ)
        slot = r_in.at[zz if arriving else z]
        return remote(r_out, slot, s_p2.at[d], r_p2.at[d], dev(zz, y, c, x))

    def send_3(d, arriving):
        yy = down(y, d, NY) if arriving else up(y, d, NY)
        slot = pf.at[yy if arriving else y]
        return remote(f_out.at[yy], slot, s_p3.at[d], r_p3.at[d], dev(z, yy, c, x))

    def at_copy(h, who):
        ref = attn.at[pl.ds(pl.multiple_of(who * HALF + h * HD, HD), HD)]
        return remote(ref, ref, s_at.at[h], r_at.at[h], sibling)

    def turn(tokens):
        fk_s[tokens] = feature(kx[tokens])
        v_t[:, tokens] = vx[tokens].T

    def states():
        for copy in inputs:
            copy.wait()
        turn(mine)
        fq_t[:, mine] = feature(qx[mine]).T
        qkv_in[0].wait_recv()
        qkv_in[1].wait_recv()
        turn(other)
        for h in range(HEADS):
            hs = slice(h * HD, (h + 1) * HD)
            state = dot(v_t[hs], fk_s[:, hs]).astype(BF16)
            s_out[2 * h] = state[:SL]
            s_out[2 * h + 1] = state[SL:]

        for d in FAR_FIRST:
            send_1(d, False).start()

        s_in[y] = s_out[y]

    def queries():
        qkv_in[2].wait_recv()
        fq_t[:, other] = feature(qx[other]).T

    def inside(h):
        keys_at = lax.broadcasted_iota(jnp.int32, (2 * TOK, 2 * TOK), 0)
        query_at = lax.broadcasted_iota(jnp.int32, (2 * TOK, 2 * TOK), 1)
        hs = slice(h * HD, (h + 1) * HD)
        scores = dot(fk_s[:, hs], fq_t[hs])
        weights = jnp.where(keys_at <= query_at, scores, 0.0).astype(BF16)
        mixed[hs] = dot(v_t[hs], weights)

    def row_prefix():
        for d in FAR_FIRST:
            send_1(d, True).wait_recv()

        run = jnp.zeros((SL, HD), F32)
        for i in range(NY):
            e_buf[i] = run
            run = run + s_in[i].astype(F32)
        r_out[...] = run.astype(BF16)

        for d in FAR_FIRST:

            @pl.when(z + d < NZ)
            def _():
                send_2(d, False).start()

        r_in[z] = r_out[...]

    def all_prefix():
        for d in FAR_FIRST:

            @pl.when(z >= d)
            def _():
                send_2(d, True).wait_recv()

        before = jnp.zeros((SL, HD), F32)
        for i in range(NZ):
            before = before + jnp.where(i < z, r_in[i].astype(F32), 0.0)
        for i in range(NY):
            f_out[i] = (before + e_buf[i]).astype(BF16)

        for d in FAR_FIRST:
            send_3(d, False).start()

        pf[y] = f_out[y]

    def attend():
        gains = []
        for h in range(HEADS):
            at = pl.ds(pl.multiple_of(c * HALF + h * HD, HD), HD)
            turned = jnp.broadcast_to(gain[:, at], (HD, HD)).T
            gains.append(jnp.concatenate([turned, turned], axis=1))

        for d in FAR_FIRST:
            send_3(d, True).wait_recv()

        for h in range(HEADS):
            hs = slice(h * HD, (h + 1) * HD)
            at = pl.ds(pl.multiple_of(c * HALF + h * HD, HD), HD)
            prefix = pf[2 * h : 2 * h + 2].reshape(HD, HD)
            total = mixed[hs] + dot(prefix, fq_t[hs])
            scale = lax.rsqrt(jnp.mean(total * total, axis=0, keepdims=True) + 1e-05)
            attn[at] = (total * scale * gains[h]).astype(BF16)
            at_copy(h, c).start()

    def unit_a(i):
        zz = up(z, jnp.where(lax.rem(i, 2) == 1, lax.div(i + 1, 2), NZ - lax.div(i, 2)), NZ)
        return zz, lax.div(zz, 2), 0, lax.rem(zz, 2), lambda: wa[zz].reshape(NY * WB, 2 * HALF)

    def unit_b(rel, grp):
        xx = up(x, rel, NX)

        def blocks():
            found = []
            for zl in range(2):
                d = up(2 * xx + zl, NZ - z, NZ)
                slot = jnp.where(d <= 4, jnp.maximum(2 * d - 1, 0), 2 * NZ - 2 * d)
                for off in ORDER[4 * grp : 4 * grp + 4]:
                    found.append(wb[up(y, off % NY, NY), slot])
            return jnp.concatenate(found, axis=0)

        return NZ + 2 * xx + grp, xx, 1, grp, blocks

    def far_copy(n, i):
        rows = pl.ds(i * SL, SL)
        to = dev(z, y, c, x_dn if i else x_up)
        return remote(near.at[n, :, rows], got.at[n, i], s_far.at[n, i], r_far.at[n, i], to)

    def rows_of(half):
        return pl.ds(pl.multiple_of(half * SL, SL), SL)

    def near_copy(n, kind, idx, way, core, half):
        to = dev(z, y, core, jnp.where(way == 0, x_up, x_dn))
        rows = rows_of(half)
        return remote(
            near.at[n, core, rows], fin.at[c, kind, idx, way, rows], s_near.at[n, core, half],
            r_fin.at[((c * 2 + kind) * 2 + idx) * 2 + way, half], to,
        )

    def sib_copy(n, kind, idx):
        i = kind * 2 + idx
        return remote(near.at[n, 1 - c], sib.at[i], s_near.at[n, 0, 0], r_sib.at[i], sibling)

    def far_unit(n, xx, kind, idx, blocks):
        @pl.when(up(xx, NX - x, NX) == 2)
        def _():
            total = dot(blocks(), attn[...]).astype(BF16)
            for core in range(2):
                near[n, core] = total[:, core * TOK : (core + 1) * TOK]
            for i in range(2):
                far_copy(n, i).start()

    def near_unit(n, xx, kind, idx, blocks):
        rel = up(xx, NX - x, NX)

        @pl.when(lax.rem(rel, 2) == 1)
        def _():
            total = dot(blocks(), attn[...])
            way = lax.div(rel, 2)
            for core in range(2):
                part[core] = total[:, core * TOK : (core + 1) * TOK]
                near[n, core] = part[core].astype(BF16)
                keep[n, core] = part[core, rows_of(way)]
                near_copy(n, kind, idx, way, core, 1 - way).start()

        @pl.when(rel == 0)
        def _():
            total = dot(blocks(), attn[...]).astype(BF16)
            for core in range(2):
                near[n, core] = total[:, core * TOK : (core + 1) * TOK]
            sib_copy(n, kind, idx).start()

    def sum_unit(n, xx, kind, idx, blocks):
        rel = up(xx, NX - x, NX)

        @pl.when(lax.rem(rel, 2) == 1)
        def _():
            way = lax.div(rel, 2)
            ref = got.at[n, way]
            remote(ref, ref, s_far.at[n, way], r_far.at[n, way], sibling).wait_recv()
            for core in range(2):
                near[n, core, rows_of(way)] = (keep[n, core] + got[n, way, core].astype(F32)).astype(BF16)
                near_copy(n, kind, idx, way, core, way).start()

    def far_units(first, last, grp):
        @pl.loop(first, last)
        def _(i):
            far_unit(*unit_a(i))

        far_unit(*unit_b(2, grp))

    def near_units(first, last, grp):
        @pl.loop(first, last)
        def _(i):
            near_unit(*unit_a(i))

        for rel in (1, 3, 0):
            near_unit(*unit_b(rel, grp))

    def sum_units(first, last, grp):
        @pl.loop(first, last)
        def _(i):
            sum_unit(*unit_a(i))

        for rel in (1, 3):
            sum_unit(*unit_b(rel, grp))

    def line_1():
        line_recv(1)
        ring_send(1, 1)

    def line_2():
        line_recv(2)
        line_send(3)
        line_send(4)
        ring_send(1, 2)

    def line_3():
        line_recv(3)
        ring_send(1, 3)
        line_recv(4)
        ring_send(1, 4)

    def swap():
        for h in range(HEADS):
            at_copy(h, 1 - c).wait_recv()

    def early_far():
        far_units(0, 5, 0)

    def early_near():
        near_units(0, 5, 0)

    def late_far():
        far_units(5, NZ, 1)

    def late_near():
        near_units(5, NZ, 1)

    def early_sum():
        sum_units(0, 5, 0)

    def late_sum():
        sum_units(5, NZ, 1)

    def rings(*pairs):
        for pair in pairs:
            ring_recv(*pair)

    states()
    line_1()
    queries()
    line_2()
    ring_recv(1, 1, (0,))
    ring_recv(1, 1, (1,))
    inside(0)
    line_3()
    ring_recv(1, 2, (0,))
    ring_recv(1, 2, (1,))
    inside(1)
    row_prefix()
    ring_recv(1, 3, (0,))
    ring_recv(1, 3, (1,))
    ring_recv(1, 4, (0,))
    inside(2)
    ring_recv(1, 0, (0,))
    ring_recv(1, 4, (1,))
    inside(3)
    ring_recv(1, 0, (1,))
    ring_recv(2, 1, (0,))
    ring_recv(2, 1, (1,))
    all_prefix()
    ring_recv(2, 2, (0,))
    ring_recv(2, 3, (0,))
    ring_recv(2, 2, (1,))
    ring_recv(2, 3, (1,))
    ring_recv(2, 4, (0,))
    ring_recv(2, 4, (1,))
    ring_recv(3, 1, (0,))
    ring_recv(3, 1, (1,))
    ring_recv(2, 0, (0,))
    ring_recv(2, 0, (1,))
    attend()
    ring_recv(3, 2, (0,))
    ring_recv(3, 2, (1,))
    ring_recv(3, 3, (0,))
    ring_recv(3, 3, (1,))
    ring_recv(3, 4, (0,))
    ring_recv(3, 4, (1,))
    ring_recv(3, 0, (0,))
    ring_recv(3, 0, (1,))
    swap()
    early_far()
    early_near()
    ring_recv(4, 1, (0,))
    ring_recv(4, 1, (1,))
    ring_recv(4, 2, (0,))
    ring_recv(4, 2, (1,))
    ring_recv(4, 0, (0,))
    ring_recv(4, 0, (1,))
    ring_recv(4, 3, (0,))
    ring_recv(4, 3, (1,))
    ring_recv(4, 4, (0,))
    ring_recv(4, 4, (1,))
    late_far()
    early_sum()
    late_near()
    late_sum()
    for kind, idx in ((1, 0), (0, 0), (0, 1), (1, 1)):
        n = 2 * x + idx + kind * NZ
        away = sib.at[kind * 2 + idx]
        remote(away, away, s_near.at[0, 0, 0], r_sib.at[kind * 2 + idx], sibling).wait_recv()
        for s in range(2):
            for way in range(2):
                i = ((s * 2 + kind) * 2 + idx) * 2 + way
                for half in range(2):
                    ref = fin.at[s, kind, idx, way, pl.ds(half * SL, SL)]
                    remote(ref, ref, s_near.at[0, 0, 0], r_fin.at[i, half], sibling).wait_recv()
            own = jnp.where(s == c, near[n, c].astype(F32), sib[kind * 2 + idx].astype(F32))
            total = own + fin[s, kind, idx, 0].astype(F32) + fin[s, kind, idx, 1].astype(F32)
            for i in range(NY):
                zl, off = (idx, ORDER[i]) if kind == 0 else (i // 4, ORDER[4 * idx + i % 4])
                out_t[zl * NY + up(y, off % NY, NY), 2 * s + kind] = total[i * WB : (i + 1) * WB]
    for j in range(NY):
        o_ref[:, j * HD : (j + 1) * HD] = out_t[2 * j : 2 * j + 2].reshape(HD, HD).T.astype(BF16)

    for copy in qkv:
        copy.wait_send()

    @pl.loop(1, NY)
    def _(d):
        send_1(d, False).wait_send()
        send_3(d, False).wait_send()

        @pl.when(z + d < NZ)
        def _():
            send_2(d, False).wait_send()

    for kind, way in both:
        for k in range(1, 5):
            if k < 4 or kind == way:
                line(kind, way, k, False).wait_send()
        for step in range(1, 5):
            for group in range(5):
                if step < 4 or group in LAST[kind][way]:
                    ring(kind, way, step, group, False).wait_send()
    for h in range(HEADS):
        at_copy(h, c).wait_send()

    def unit_left(n, xx, kind, idx, blocks):
        rel = up(xx, NX - x, NX)

        @pl.when(rel == 2)
        def _():
            for i in range(2):
                far_copy(n, i).wait_send()

        @pl.when(lax.rem(rel, 2) == 1)
        def _():
            for core in range(2):
                for half in range(2):
                    near_copy(n, kind, idx, lax.div(rel, 2), core, half).wait_send()

        @pl.when(rel == 0)
        def _():
            sib_copy(n, kind, idx).wait_send()

    @pl.loop(0, NZ)
    def _(i):
        unit_left(*unit_a(i))

    for rel in range(NX):
        for grp in range(2):
            unit_left(*unit_b(rel, grp))


def per_device(queries, keys, values, head_gain, w_out):
    dma = pltpu.SemaphoreType.DMA
    vmem = pltpu.VMEM
    rows = NY * WB
    scratch = [
        vmem((1, 2 * HALF), F32),
        vmem((NZ, NY, WB, 2 * HALF), BF16),
        vmem((NY, NZ, WB, 2 * HALF), BF16),
        vmem((2 * TOK, HALF), BF16),
        vmem((2 * TOK, HALF), BF16),
        vmem((2 * TOK, HALF), BF16),
        vmem((HALF, 2 * TOK), BF16),
        vmem((2 * TOK, HALF), BF16),
        vmem((HALF, 2 * TOK), BF16),
        vmem((NY, SL, HD), BF16),
        vmem((NY, SL, HD), BF16),
        vmem((NY, SL, HD), F32),
        vmem((SL, HD), BF16),
        vmem((NZ, SL, HD), BF16),
        vmem((NY, SL, HD), BF16),
        vmem((NY, SL, HD), BF16),
        vmem((HALF, 2 * TOK), F32),
        vmem((2 * HALF, 2 * TOK), BF16),
        vmem((16, 2, rows, TOK), BF16),
        vmem((16, 2, 2, SL, TOK), BF16),
        vmem((2, 2, 2, 2, rows, TOK), BF16),
        vmem((4, rows, TOK), BF16),
        vmem((2, rows, TOK), F32),
        vmem((16, 2, SL, TOK), F32),
        vmem((2 * NY, 4, WB, TOK), F32),
        dma((6,)),
        dma((3,)), dma((3,)),
        dma((16,)), dma((16,)), dma((80,)), dma((80,)),
        dma((8,)), dma((8,)), dma((8,)), dma((8,)), dma((8,)), dma((8,)),
        dma((HEADS,)), dma((HEADS,)),
        dma((16, 2)), dma((16, 2)), dma((16, 2, 2)),
        dma((16, 2)), dma((4,)),
    ]
    operands = (queries, keys, values, head_gain.reshape(1, -1), w_out.T)
    return pl.pallas_call(
        kernel,
        out_shape=jax.ShapeDtypeStruct(queries.shape, BF16),
        in_specs=[pl.BlockSpec(memory_space=pl.ANY)] * 5,
        out_specs=pl.BlockSpec(memory_space=pltpu.VMEM),
        scratch_shapes=scratch,
        compiler_params=pltpu.CompilerParams(
            collective_id=0, has_side_effects=True, vmem_limit_bytes=48 * 2**20
        ),
        cost_estimate=pl.CostEstimate(flops=2**31, bytes_accessed=2**21, transcendentals=2**19),
    )(*[pltpu.with_memory_space_constraint(a, pltpu.HBM) for a in operands])


def solution(mesh):
    placed = (P("ctx", "head"), P("ctx", "head"), P("ctx", "head"), P("head"), P("head", "ctx"))
    return jax.shard_map(
        per_device, mesh=mesh, in_specs=placed, out_specs=P("ctx", "head"), check_vma=False
    )
```
